32 devices in a mesh: copies: 2 (over y), users: 4 (over z), items: 4 (over x, core).
Axes of the slice: x: 2, y: 2, z: 4, core: 2. Of those that a mesh axis runs over, the one named last changes fastest.
Arguments:
- ratings: float32 [16384, 2048], P(('copies', 'users'), 'items'), parts along dimension 0, may hold values from -6 to 6
- entry_mask: int32 [16384, 2048], P(('copies', 'users'), 'items'), parts along dimension 0, may hold values 0 or 1
- pattern: int32 [128, 16], P(('copies', 'users'), 'items'), parts along dimension 0, may hold values from 0 to 1, as said below
- left: float32 [16384, 64], P(('copies', 'users')), parts along dimension 0, may hold values from -1.5 to 1.5
- left_dir: float32 [16384, 64], P(('copies', 'users')), parts along dimension 0, may hold values from -1.5 to 1.5
- right: float32 [4096, 64], P(('copies', 'items', 'users')), parts along dimension 0, may hold values from -3 to 3
- right_dir: float32 [4096, 64], P(('copies', 'items', 'users')), parts along dimension 0, may hold values from -3 to 3
Outputs:
- grad_left: float32 [16384, 64], P(('copies', 'users')), parts along dimension 0
- hess_left: float32 [16384, 64], P(('copies', 'users')), parts along dimension 0
- grad_right: float32 [4096, 64], P(('copies', 'items', 'users')), parts along dimension 0
- hess_right: float32 [4096, 64], P(('copies', 'items', 'users')), parts along dimension 0
- inner: float32 [4], P('copies'), parts along dimension 0
The draws below stay inside these ranges and needn't reach their ends.
There are 2 independent parts, one for each index of `copies`. The reference program is written for one: setup_inputs(seed, part) draws one part's arguments, and reference() takes and returns one part's arrays. A program takes and returns all parts, laid end to end along the dimension named above; each array names one. Nothing has to cross between parts.
Inputs may be any that keep to these rules, and one draw needn't show every extreme that they name: `pattern`: 1 marks an observed tile; the share of observed tiles differs between user tiles.
All inputs are finite; a program needn't handle non-finite values. No bound on the sum of `entry_mask` on one device may be relied on, other than what follows from the above.
Results may differ from the reference program's by a relative error of at most 0.00007.
Values sent between devices are 32-bit elements; how exact they have to be, the bound alone decides.
No kernel may reach another device: no remote copies, remote signals or barrier semaphores. Data moves between devices by JAX's collectives and lax.ppermute only.
A program may use at most 64 MiB of HBM per device.

```python
import jax
import jax.numpy as jnp
from jax import lax

RANK = 64
TILE = 128
USERS = 8192
ITEMS = 2048
NUB = 64
NIB = 16


def draw_pattern(key, part):
    key = jax.random.fold_in(key, 7)
    rows = jnp.arange(NUB, dtype=jnp.int32)[:, None]
    limit = 15 + 70 * rows // max(NUB - 1, 1)
    votes = jax.random.randint(key, (NUB, NIB), 0, 100, dtype=jnp.int32)
    return (votes < limit).astype(jnp.int32)


def set_ends(drawn, key, low, largest):
    spot = [jax.random.randint(jax.random.fold_in(key, axis), (), 0, length) for axis, length in enumerate(drawn.shape)]
    widest = drawn.shape.index(max(drawn.shape))
    next_to = spot[:widest] + [(spot[widest] + 1) % drawn.shape[widest]] + spot[widest + 1:]
    return drawn.at[tuple(spot)].set(low).at[tuple(next_to)].set(largest)


def block_scale(rng, shape, shards, smallest, largest):
    level = 1.0
    for position, shards_of in shards:
        steps = jax.random.uniform(jax.random.fold_in(jax.random.fold_in(rng, 6), position), (shards_of,), jnp.float32, smallest / len(shards), largest / len(shards))
        level = level * jnp.repeat(jnp.exp(steps), shape[position] // shards_of).reshape((-1,) + (1,) * (len(shape) - 1 - position))
    return level


def bell_draw(key, dims, deviation, most, pieces=(), kind=jnp.bfloat16):
    values = deviation * jax.random.normal(key, dims, jnp.float32)
    if pieces:
        values = values * block_scale(key, dims, pieces, -0.22, 0.18)
    return jnp.clip(values, -most, most).astype(kind)


def setup_inputs(seed: int = 0, part: int = 0) -> dict:
    arg_keys = jax.random.split(jax.random.key(seed), 8)
    part_splits = jax.random.split(jax.random.fold_in(arg_keys[7], part), 8)
    ratings = bell_draw(part_splits[0], (USERS, ITEMS), 1.0, 6.0, ((0, 4), (1, 4)), jnp.float32)
    entry_mask = set_ends((jax.random.randint(part_splits[1], (USERS, ITEMS), 0, 2) < 1).astype(jnp.int32), jax.random.fold_in(part_splits[1], 1), 0, 1)
    pattern = draw_pattern(jax.random.fold_in(jax.random.fold_in(arg_keys[7], part), 71), part)
    left = bell_draw(part_splits[3], (USERS, RANK), 0.25, 1.5, ((0, 4),), jnp.float32)
    left_dir = bell_draw(part_splits[4], (USERS, RANK), 0.25, 1.5, ((0, 4),), jnp.float32)
    right = bell_draw(part_splits[5], (ITEMS, RANK), 0.5, 3.0, ((0, 16),), jnp.float32)
    right_dir = bell_draw(part_splits[6], (ITEMS, RANK), 0.5, 3.0, ((0, 16),), jnp.float32)
    return dict(ratings=ratings, entry_mask=entry_mask, pattern=pattern, left=left, left_dir=left_dir, right=right, right_dir=right_dir)


def mult(a, b):
    return jnp.dot(a, b, precision=lax.Precision.HIGHEST, preferred_element_type=jnp.float32)


def reference(ratings, entry_mask, pattern, left, left_dir, right, right_dir):
    tiles = jnp.repeat(jnp.repeat(pattern, TILE, axis=0), TILE, axis=1)
    observed = entry_mask.astype(jnp.float32) * tiles.astype(jnp.float32)
    res = observed * (mult(left, right.T) - ratings)
    change = observed * (mult(left_dir, right.T) + mult(left, right_dir.T))
    grad_left = mult(res, right) / 64.0
    grad_right = mult(res.T, left) / 64.0
    hess_left = (mult(change, right) + mult(res, right_dir)) / 64.0
    hess_right = (mult(change.T, left) + mult(res.T, left_dir)) / 64.0
    gnorm = jnp.sum(grad_left * grad_left) + jnp.sum(grad_right * grad_right)
    curve = jnp.sum(left_dir * hess_left) + jnp.sum(right_dir * hess_right)
    inner = jnp.stack([gnorm, curve]).astype(jnp.float32)
    return grad_left, hess_left, grad_right, hess_right, inner
```

```python
import functools

import jax
import jax.numpy as jnp
from jax import lax
from jax.experimental import pallas as pl
from jax.experimental.pallas import tpu as pltpu
from jax.sharding import PartitionSpec as P

F32 = jnp.float32
BF16 = jnp.bfloat16
SMEM = pl.BlockSpec(memory_space=pltpu.SMEM)


def dot(a, b):
    return jnp.dot(a, b, preferred_element_type=F32)


def halves(x):
    high = x.astype(BF16)
    return high, (x - high.astype(F32)).astype(BF16)


def tile_sum(x):
    total = jnp.sum(x, axis=0, keepdims=True)
    return functools.reduce(jnp.add, [total[:, i : i + 128] for i in range(0, total.shape[1], 128)])


def main_kernel(blocks, tile, scale, where, pattern, ratings, mask, left, left_dir, *refs):
    panels, refs = refs[:blocks], refs[blocks:]
    keep, send, curve, items = refs[0], refs[1], refs[2], refs[3 : 3 + blocks]
    forward, forward_low, back = refs[3 + blocks :]
    step = pl.program_id(0)
    rank, rows = left.shape
    wide = panels[0].shape[1]
    half = rank // 2
    flip = where[blocks] == 1

    def own_first(x):
        return jnp.where(flip, jnp.concatenate([x[half:], x[:half]], axis=0), x)

    @pl.when(step == 0)
    def _():
        for k in range(blocks):
            p, d = panels[k][:rank], panels[k][rank:]
            zero = jnp.zeros_like(p)
            q = jnp.concatenate(
                [jnp.concatenate([p, d], axis=1), jnp.concatenate([zero, p], axis=1)], axis=0
            )
            high, low = halves(q)
            forward[k, : 2 * rank] = high
            forward[k, 2 * rank :] = high
            forward_low[k] = low
            p, d, zero = own_first(p), own_first(d), zero[:half]
            s = jnp.concatenate(
                [
                    jnp.concatenate([p[:half], zero], axis=1),
                    jnp.concatenate([d[:half], p[:half]], axis=1),
                    jnp.concatenate([p[half:], zero], axis=1),
                    jnp.concatenate([d[half:], p[half:]], axis=1),
                ],
                axis=0,
            ).T
            high, low = halves(s)
            back[k, :, : 2 * rank] = high
            back[k, :, 2 * rank :] = low
            items[k][...] = jnp.zeros_like(items[k])
        curve[...] = jnp.zeros_like(curve)

    both = jnp.concatenate([left[...], left_dir[...]], axis=0)
    high, low = halves(both)
    factors = jnp.concatenate([high, low], axis=0)
    high_t, low_t = halves(both.T)
    factors_t = jnp.concatenate([high_t, low_t], axis=1)
    total = None
    for k in range(blocks):
        columns = pl.ds(pl.multiple_of(where[k] * wide, wide), wide)
        raw = dot(factors_t, forward[k]) + dot(high_t, forward_low[k])
        seen = mask[:, columns].astype(F32)
        seen = jnp.concatenate(
            [
                seen[t * tile : (t + 1) * tile]
                * (pattern[step * (rows // tile) + t, where[k]].astype(F32) * scale)
                for t in range(rows // tile)
            ],
            axis=0,
        )
        res = seen * (raw[:, :wide] - ratings[:, columns])
        change = seen * raw[:, wide:]
        rc_high, rc_low = halves(jnp.concatenate([res, change], axis=1))
        out = dot(rc_high, back[k])
        out = out[:, : 2 * rank] + out[:, 2 * rank :] + dot(rc_low, back[k, :, : 2 * rank])
        total = out if total is None else total + out
        got = dot(factors, rc_high)
        got = got[: 2 * rank] + got[2 * rank :] + dot(high, rc_low)
        items[k][:rank] += got[:rank, :wide]
        items[k][rank:] += got[:rank, wide:] + got[rank:, :wide]
    user = total.T
    keep[...] = user[:rank]
    send[...] = user[rank:]
    turned = own_first(left_dir[...])
    curve[...] += tile_sum(turned[:half] * user[half:rank] + turned[half:] * user[rank + half :])

    @pl.when(step == pl.num_programs(0) - 1)
    def _():
        for k in range(blocks):
            curve[...] += tile_sum(items[k][rank:] * panels[k][rank:])


def main_call(where, pattern, ratings, mask, left, left_dir, panels):
    users, width = ratings.shape
    rank = left.shape[0]
    blocks, wide = len(panels), panels[0].shape[1]
    rows = 256
    whole = lambda shape: pl.BlockSpec(shape, lambda i: (0,) * len(shape))
    row_block = pl.BlockSpec((rows, width), lambda i: (i, 0))
    column_block = pl.BlockSpec((rank, rows), lambda i: (0, i))
    shape = jax.ShapeDtypeStruct
    out = pl.pallas_call(
        functools.partial(main_kernel, blocks, users // pattern.shape[0], 1.0 / 64.0),
        grid=(users // rows,),
        in_specs=[SMEM, SMEM, row_block, row_block, column_block, column_block]
        + [whole((2 * rank, wide))] * blocks,
        out_specs=[column_block, column_block, whole((1, 128))] + [whole((2 * rank, wide))] * blocks,
        out_shape=[shape((rank, users), F32), shape((rank, users), F32), shape((1, 128), F32)]
        + [shape((2 * rank, wide), F32)] * blocks,
        scratch_shapes=[
            pltpu.VMEM((blocks, 4 * rank, 2 * wide), BF16),
            pltpu.VMEM((blocks, 2 * rank, 2 * wide), BF16),
            pltpu.VMEM((blocks, 2 * wide, 4 * rank), BF16),
        ],
        compiler_params=pltpu.CompilerParams(vmem_limit_bytes=48 * 1024 * 1024),
        cost_estimate=pl.CostEstimate(
            flops=2 * users * width * rank * 54, bytes_accessed=10 * users * width, transcendentals=0
        ),
        name="main",
    )(where, pattern, ratings, mask, left, left_dir, *panels)
    return out[0], out[1], out[2], out[3:]


def items_kernel(count, *refs):
    terms, (curve, grad, hess, sums) = refs[:count], refs[count:]
    total = functools.reduce(jnp.add, [t[...] for t in terms])
    rank = total.shape[0] // 2
    grad[...] = total[:rank]
    hess[...] = total[rank:]
    squares = jnp.sum(total[:rank] * total[:rank], axis=0, keepdims=True)
    wide = squares.shape[1]
    if wide < 128:
        squares = jnp.concatenate([squares, jnp.zeros((1, 128 - wide), F32)], axis=1)
    sums[...] = jnp.concatenate([squares, curve[...], jnp.zeros((6, 128), F32)], axis=0)


def items_call(terms, curve):
    rows, wide = terms[0].shape
    shape = jax.ShapeDtypeStruct
    return pl.pallas_call(
        functools.partial(items_kernel, len(terms)),
        out_shape=[shape((rows // 2, wide), F32), shape((rows // 2, wide), F32), shape((8, 128), F32)],
        name="items_total",
    )(*terms, curve)


def squares_kernel(a, b, sums, total, new):
    x = a[...] + b[...]
    total[...] = x
    new[...] = sums[...]
    new[0:1] += tile_sum(x * x)


def squares_call(a, b, sums):
    shape = jax.ShapeDtypeStruct
    return pl.pallas_call(
        squares_kernel,
        out_shape=[shape(a.shape, F32), shape(sums.shape, F32)],
        name="squares",
    )(a, b, sums)


def swap(x, axis, bit):
    return lax.ppermute(x, axis, [(i, i ^ bit) for i in range(lax.axis_size(axis))])


def bits(axis):
    return [1 << i for i in range(lax.axis_size(axis).bit_length() - 1)]


def per_device(ratings, entry_mask, pattern, left, left_dir, right, right_dir):
    rank = left.shape[1]
    wide = right.shape[0]
    n = lax.axis_size("users")
    me = lax.axis_index("users")
    core = lax.axis_index("items") % 2
    own = jnp.concatenate([right.T, right_dir.T], axis=0)
    direct = wide == 128
    if direct:
        panels = [own] + [swap(own, "users", k) for k in range(1, n)]
        index = [me ^ k for k in range(n)]
    else:
        panel = lax.all_gather(own, "users", axis=1, tiled=True)
        panels = [panel[:, i : i + 128] for i in range(0, panel.shape[1], 128)]
        index = list(range(len(panels)))
    where = jnp.stack([jnp.asarray(i, jnp.int32) for i in index + [core]])
    keep, send, curve, items = main_call(
        where, pattern, ratings, entry_mask, left.T, left_dir.T, panels
    )
    got = swap(send, "items", 1)
    half = rank // 2
    g = keep[:half] + got[:half]
    h = keep[half:] + got[half:]
    if direct:
        terms = [items[0]] + [swap(items[k], "users", k) for k in range(1, n)]
    else:
        terms = [
            lax.psum_scatter(jnp.concatenate(items, axis=1), "users", scatter_dimension=1, tiled=True)
        ]
    grad_right, hess_right, sums = items_call(terms, curve)
    across = bits("items")[1:]
    for bit in across:
        sums = sums + swap(sums, "items", bit)
    for bit in across[:-1]:
        g = g + swap(g, "items", bit)
        h = h + swap(h, "items", bit)
    other_g = swap(g, "items", across[-1])
    other_h = swap(h, "items", across[-1])
    g, sums = squares_call(g, other_g, sums)
    h = h + other_h
    for bit in bits("users"):
        sums = sums + swap(sums, "users", bit)
    sums = sums + swap(sums, "items", 1)
    inner = jnp.sum(sums[:2], axis=1)

    def joined(mine):
        other = swap(mine, "items", 1)
        return jnp.concatenate([jnp.where(core == 0, mine, other), jnp.where(core == 0, other, mine)], axis=0)

    return joined(g).T, joined(h).T, grad_right.T, hess_right.T, inner


def solution(mesh):
    placed = (
        P(("copies", "users"), "items"),
        P(("copies", "users"), "items"),
        P(("copies", "users"), "items"),
        P(("copies", "users"), None),
        P(("copies", "users"), None),
        P(("copies", "items", "users"), None),
        P(("copies", "items", "users"), None),
    )
    return jax.shard_map(
        per_device,
        mesh=mesh,
        in_specs=placed,
        out_specs=(
            P(("copies", "users"), None),
            P(("copies", "users"), None),
            P(("copies", "items", "users"), None),
            P(("copies", "items", "users"), None),
            P("copies"),
        ),
        check_vma=False,
    )
```

```python
import functools
import itertools
import jax
import jax.numpy as jnp
from jax import lax
from jax.experimental import pallas as pl
from jax.experimental.pallas import tpu as pltpu
from jax.sharding import PartitionSpec as P

F32 = jnp.float32
BF16 = jnp.bfloat16
SMEM = pl.BlockSpec(memory_space=pltpu.SMEM)
VMEM = pl.BlockSpec(memory_space=pltpu.VMEM)
HBM = pl.BlockSpec(memory_space=pltpu.HBM)


def dot(a, b):
    return jnp.dot(a, b, preferred_element_type=F32)


def halves(x):
    high = x.astype(BF16)
    return high, (x - high.astype(F32)).astype(BF16)


def tile_sum(x):
    total = jnp.sum(x, axis=0, keepdims=True)
    return functools.reduce(jnp.add, [total[:, i : i + 128] for i in range(0, total.shape[1], 128)])


def first_loads(where, rows, factors, factors_to, factor_sems, grids, grids_to, own_sems, other_sems):
    users, width = grids[0].shape
    wide = 128
    block = lambda k: pl.ds(pl.multiple_of(where[k] * wide, wide), wide)
    steps = []
    for step in range(users // rows):
        here = pl.ds(step * rows, rows)
        steps.append(
            [
                pltpu.make_async_copy(a.at[:, here], b.at[:, here], factor_sems.at[i, step])
                for i, (a, b) in enumerate(zip(factors, factors_to))
            ]
            + [
                pltpu.make_async_copy(a.at[here, block(0)], b.at[here, block(0)], own_sems.at[i, step])
                for i, (a, b) in enumerate(zip(grids, grids_to))
            ]
        )
    rest = [
        pltpu.make_async_copy(a.at[:, block(k)], b.at[:, block(k)], other_sems.at[i, k - 1])
        for k in range(1, width // wide)
        for i, (a, b) in enumerate(zip(grids, grids_to))
    ]
    return steps, rest


def block_kernel(blocks, first, last, span, rows, tile, loop, where, pattern, ratings, mask, *refs):
    refs = list(refs)
    take = lambda n: [refs.pop(0) for _ in range(n)]
    if first:
        left_hbm, left_dir_hbm = take(2)
    else:
        factors_t, factors, acc = take(3)
        left_dir = take(1)[0] if last else None
    panels = take(blocks)
    start, stop = span
    items_in = take(blocks) if last and start > 0 else None
    if first:
        factors_t, factors, ratings_hbm, mask_hbm = *take(2), ratings, mask
        ratings, mask, left_dir = take(3)
    if last:
        keep, send = take(2)
    else:
        acc_out = take(1)[0]
    curve = take(1)[0]
    items = take(blocks)
    forward, forward_low, back = take(3)
    if first:
        left, factor_sems, own_sems, other_sems = refs
        loads = first_loads(
            where, rows, (left_hbm, left_dir_hbm), (left, left_dir), factor_sems,
            (ratings_hbm, mask_hbm), (ratings, mask), own_sems, other_sems,
        )
        for copy in itertools.chain(*loads[0], loads[1]):
            copy.start()
    rank2, wide = panels[0].shape
    rank = rank2 // 2
    half = rank // 2
    flip = where[ratings.shape[1] // wide if first else blocks] == 1

    def own_first(x):
        return jnp.where(flip, jnp.concatenate([x[half:], x[:half]], axis=0), x)

    for k in range(blocks):
        p, d = panels[k][:rank], panels[k][rank:]
        zero = jnp.zeros_like(p)
        q = jnp.concatenate([jnp.concatenate([p, d], axis=1), jnp.concatenate([zero, p], axis=1)], axis=0)
        high, low = halves(q)
        forward[k, : 2 * rank] = high
        forward[k, 2 * rank :] = high
        forward_low[k] = low
        p, d, zero = own_first(p), own_first(d), zero[:half]
        s = jnp.concatenate(
            [
                jnp.concatenate([p[:half], zero], axis=1),
                jnp.concatenate([d[:half], p[:half]], axis=1),
                jnp.concatenate([p[half:], zero], axis=1),
                jnp.concatenate([d[half:], p[half:]], axis=1),
            ],
            axis=0,
        ).T
        high, low = halves(s)
        back[k, :, : 2 * rank] = high
        back[k, :, 2 * rank :] = low
        items[k][...] = jnp.zeros_like(items[k]) if items_in is None else items_in[k][...]
    curve[...] = jnp.zeros_like(curve)

    def do(step):
        here = pl.ds(step if isinstance(step, int) else pl.multiple_of(step, rows), rows)
        if first:
            for copy in loads[0][step // rows]:
                copy.wait()
            both = jnp.concatenate([left[:, here], left_dir[:, here]], axis=0)
            high, low = halves(both)
            factors[: 2 * rank, here] = high
            factors[2 * rank :, here] = low
            high_t, low_t = halves(both.T)
            factors_t[here, : 2 * rank] = high_t
            factors_t[here, 2 * rank :] = low_t
            total = None
        else:
            total = acc[here, :]
        for k in range(blocks):
            columns = pl.ds(pl.multiple_of(where[k] * wide, wide), wide)
            raw = dot(factors_t[here, :], forward[k]) + dot(factors_t[here, : 2 * rank], forward_low[k])
            seen = mask[here, columns].astype(F32)
            seen = jnp.concatenate(
                [
                    seen[t * tile : (t + 1) * tile]
                    * (pattern[where[k], step // tile + t].astype(F32) * (1.0 / 64.0))
                    for t in range(rows // tile)
                ],
                axis=0,
            )
            res = seen * (raw[:, :wide] - ratings[here, columns])
            change = seen * raw[:, wide:]
            rc_high, rc_low = halves(jnp.concatenate([res, change], axis=1))
            out = dot(rc_high, back[k])
            out = out[:, : 2 * rank] + out[:, 2 * rank :] + dot(rc_low, back[k, :, : 2 * rank])
            total = out if total is None else total + out
            got = dot(factors[:, here], rc_high)
            got = got[: 2 * rank] + got[2 * rank :] + dot(factors[: 2 * rank, here], rc_low)
            items[k][:rank] += got[:rank, :wide]
            items[k][rank:] += got[:rank, wide:] + got[rank:, :wide]
        if last:
            user = total.T
            there = pl.ds(step - start if isinstance(step, int) else pl.multiple_of(step - start, rows), rows)
            keep[:, there] = user[:rank]
            send[:, there] = user[rank:]
            turned = own_first(left_dir[:, here])
            curve[...] += tile_sum(turned[:half] * user[half:rank] + turned[half:] * user[rank + half :])
        else:
            acc_out[here, :] = total

    if loop:
        def body(i, c):
            do(start + i * rows)
            return c
        lax.fori_loop(0, (stop - start) // rows, body, 0)
    else:
        for s in range(start, stop, rows):
            do(s)
    if first:
        for copy in loads[1]:
            copy.wait()
    if last and stop == ratings.shape[0] or not last:
        for k in range(blocks):
            curve[...] += tile_sum(items[k][rank:] * panels[k][rank:])


def block_call(where, pattern, ratings, mask, given, panels, first=False, last=False, span=None, items=(), rows=512, loop=True, name="block"):
    users, width = ratings.shape
    rank = panels[0].shape[0] // 2
    wide = panels[0].shape[1]
    blocks = len(panels)
    span = span or (0, users)
    count = span[1] - span[0]
    shape = jax.ShapeDtypeStruct
    outs = []
    scratch = [
        pltpu.VMEM((blocks, 4 * rank, 2 * wide), BF16),
        pltpu.VMEM((blocks, 2 * rank, 2 * wide), BF16),
        pltpu.VMEM((blocks, 2 * wide, 4 * rank), BF16),
    ]
    if first:
        outs += [shape((users, 4 * rank), BF16), shape((4 * rank, users), BF16)]
        outs += [shape(x.shape, x.dtype) for x in (ratings, mask, given[1])]
        steps = users // rows
        scratch += [
            pltpu.VMEM((rank, users), F32),
            pltpu.SemaphoreType.DMA((2, steps)),
            pltpu.SemaphoreType.DMA((2, steps)),
            pltpu.SemaphoreType.DMA((2, width // wide - 1)),
        ]
    outs += [shape((rank, count), F32)] * 2 if last else [shape((users, 2 * rank), F32)]
    outs += [shape((1, 128), F32)] + [shape((2 * rank, wide), F32)] * blocks
    args = [ratings, mask, *given, *panels, *items]
    far = 4 if first else 0
    args = [pltpu.with_memory_space_constraint(a, pltpu.HBM) for a in args[:far]] + [pltpu.with_memory_space_constraint(a, pltpu.VMEM) for a in args[far:]]
    return pl.pallas_call(
        functools.partial(block_kernel, blocks, first, last, span, rows, users // pattern.shape[1], loop),
        in_specs=[SMEM, SMEM] + [HBM] * far + [VMEM] * (len(args) - far),
        out_specs=[VMEM] * len(outs),
        out_shape=outs,
        scratch_shapes=scratch,
        compiler_params=pltpu.CompilerParams(vmem_limit_bytes=24 * 1024 * 1024),
        cost_estimate=pl.CostEstimate(flops=2 * count * wide * blocks * rank * 54, bytes_accessed=8 * count * wide * blocks, transcendentals=0),
        name=name,
    )(where, pattern, *args)


def items_kernel(count, *refs):
    terms, curves, (grad, hess, sums) = refs[:count], refs[count:-3], refs[-3:]
    total = functools.reduce(jnp.add, [t[...] for t in terms])
    rank = total.shape[0] // 2
    grad[...] = total[:rank]
    hess[...] = total[rank:]
    squares = jnp.sum(total[:rank] * total[:rank], axis=0, keepdims=True)
    wide = squares.shape[1]
    if wide < 128:
        squares = jnp.concatenate([squares, jnp.zeros((1, 128 - wide), F32)], axis=1)
    curve = functools.reduce(jnp.add, [c[...] for c in curves])
    sums[...] = jnp.concatenate([squares, curve, jnp.zeros((6, 128), F32)], axis=0)


def small_call(kernel, args, outs, name):
    args = [pltpu.with_memory_space_constraint(a, pltpu.VMEM) for a in args]
    return pl.pallas_call(
        kernel,
        in_specs=[VMEM] * len(args),
        out_specs=[VMEM] * len(outs),
        out_shape=[jax.ShapeDtypeStruct(o, F32) for o in outs],
        compiler_params=pltpu.CompilerParams(vmem_limit_bytes=4 * 1024 * 1024),
        name=name,
    )(*args)


def items_call(terms, curves):
    rows, wide = terms[0].shape
    return small_call(
        functools.partial(items_kernel, len(terms)),
        [*terms, *curves],
        [(rows // 2, wide), (rows // 2, wide), (8, 128)],
        "items_total",
    )


def squares_kernel(a, b, sums, total, new):
    x = a[...] + b[...]
    total[...] = x
    new[...] = sums[...]
    new[0:1] += tile_sum(x * x)


def squares_call(a, b, sums):
    return small_call(squares_kernel, [a, b, sums], [a.shape, sums.shape], "squares")


def add_kernel(a, b, after, total):
    total[...] = a[...] + b[...]


def add_call(a, b, after):
    return small_call(add_kernel, [a, b, after], [a.shape], "add")[0]


def swap(x, axis, bit):
    return lax.ppermute(x, axis, [(i, i ^ bit) for i in range(lax.axis_size(axis))])


def bits(axis):
    return [1 << i for i in range(lax.axis_size(axis).bit_length() - 1)]


def per_device(ratings, entry_mask, pattern, left, left_dir, right, right_dir):
    rank = left.shape[1]
    wide = right.shape[0]
    n = lax.axis_size("users")
    me = lax.axis_index("users")
    core = lax.axis_index("items") % 2
    own = jnp.concatenate([right.T, right_dir.T], axis=0)
    direct = wide == 128
    if direct:
        panels = [own] + [swap(own, "users", k) for k in range(1, n)]
        index = [me ^ k for k in range(n)]
    else:
        panel = lax.all_gather(own, "users", axis=1, tiled=True)
        panels = [panel[:, i : i + 128] for i in range(0, panel.shape[1], 128)]
        index = list(range(len(panels)))

    def where(blocks):
        return jnp.stack([jnp.asarray(i, jnp.int32) for i in [index[k] for k in blocks] + [core]])

    table = pattern.T
    factors_t, factors, ratings, entry_mask, left_dir_t, acc, curve_a, item = block_call(
        where(range(len(panels))), table, ratings, entry_mask, [left.T, left_dir.T], panels[:1],
        first=True, rows=1024, loop=False, name="own_block",
    )
    items = [item]
    others = list(range(1, len(panels)))
    keep, send, curve_b, *rest = block_call(
        where(others), table, ratings, entry_mask, [factors_t, factors, acc, left_dir_t], panels[1:],
        last=True, rows=1024, loop=False, name="other_blocks",
    )
    items += rest
    got = swap(send, "items", 1)
    half = rank // 2
    g = keep[:half] + got[:half]
    h = keep[half:] + got[half:]
    across = bits("items")[1:]
    for bit in across[:-1]:
        g = g + swap(g, "items", bit)
        h = h + swap(h, "items", bit)
    other_g = swap(g, "items", across[-1])
    other_h = swap(h, "items", across[-1])
    if direct:
        terms = [items[0]] + [swap(items[k], "users", k) for k in range(1, n)]
    else:
        terms = [
            lax.psum_scatter(jnp.concatenate(items, axis=1), "users", scatter_dimension=1, tiled=True)
        ]
    grad_right, hess_right, sums = items_call(terms, [curve_a, curve_b])
    for bit in across:
        sums = sums + swap(sums, "items", bit)
    g, sums = squares_call(g, other_g, sums)
    h = add_call(h, other_h, sums)
    for bit in bits("users"):
        sums = sums + swap(sums, "users", bit)
    sums = sums + swap(sums, "items", 1)
    inner = jnp.sum(sums[:2], axis=1)

    def joined(mine):
        other = swap(mine, "items", 1)
        return jnp.concatenate([jnp.where(core == 0, mine, other), jnp.where(core == 0, other, mine)], axis=0)

    return joined(g).T, joined(h).T, grad_right.T, hess_right.T, inner


def solution(mesh):
    placed = (
        P(("copies", "users"), "items"),
        P(("copies", "users"), "items"),
        P(("copies", "users"), "items"),
        P(("copies", "users"), None),
        P(("copies", "users"), None),
        P(("copies", "items", "users"), None),
        P(("copies", "items", "users"), None),
    )
    return jax.shard_map(
        per_device,
        mesh=mesh,
        in_specs=placed,
        out_specs=(
            P(("copies", "users"), None),
            P(("copies", "users"), None),
            P(("copies", "items", "users"), None),
            P(("copies", "items", "users"), None),
            P("copies"),
        ),
        check_vma=False,
    )
```

```python
import functools
import itertools
import jax
import jax.numpy as jnp
from jax import lax
from jax.experimental import pallas as pl
from jax.experimental.pallas import tpu as pltpu
from jax.sharding import PartitionSpec as P

F32 = jnp.float32
BF16 = jnp.bfloat16
SMEM = pl.BlockSpec(memory_space=pltpu.SMEM)
VMEM = pl.BlockSpec(memory_space=pltpu.VMEM)
HBM = pl.BlockSpec(memory_space=pltpu.HBM)


def dot(a, b):
    return jnp.dot(a, b, preferred_element_type=F32)


def halves(x):
    high = x.astype(BF16)
    return high, (x - high.astype(F32)).astype(BF16)


def tile_sum(x):
    total = jnp.sum(x, axis=0, keepdims=True)
    return functools.reduce(jnp.add, [total[:, i : i + 128] for i in range(0, total.shape[1], 128)])


def first_loads(where, rows, factors, factors_to, factor_sems, grids, grids_to, own_sems):
    users, width = grids[0].shape
    wide = 128
    block = lambda k: pl.ds(pl.multiple_of(where[k] * wide, wide), wide)
    steps = []
    for step in range(users // rows):
        here = pl.ds(step * rows, rows)
        steps.append(
            [
                pltpu.make_async_copy(a.at[:, here], b.at[:, here], factor_sems.at[i, step])
                for i, (a, b) in enumerate(zip(factors, factors_to))
            ]
            + [
                pltpu.make_async_copy(a.at[here, block(0)], b.at[here], own_sems.at[i, step])
                for i, (a, b) in enumerate(zip(grids, grids_to))
            ]
        )
    return steps


def other_loads(where, blocks, here, grids, grids_to, sems):
    wide = 128
    block = lambda k: pl.ds(pl.multiple_of(where[k] * wide, wide), wide)
    return [
        pltpu.make_async_copy(a.at[here, block(k)], b.at[:, block(k)], sems.at[i, j])
        for j, k in enumerate(blocks)
        for i, (a, b) in enumerate(zip(grids, grids_to))
    ]


def block_kernel(blocks, first, last, span, rows, tile, where, pattern, ratings, mask, *refs):
    refs = list(refs)
    take = lambda n: [refs.pop(0) for _ in range(n)]
    if first:
        left_hbm, left_dir_hbm = take(2)
    else:
        factors_t, factors, acc = take(3)
        left_dir = take(1)[0] if last else None
    panels = take(blocks)
    start, stop = span
    if first:
        factors_t, factors, all_ratings, all_mask, left_dir = take(5)
    if last:
        keep, send = take(2)
    else:
        acc_out = take(1)[0]
    curve = take(1)[0]
    items = take(blocks)
    forward, forward_low, back = take(3)
    if first:
        left, own_ratings, own_mask, factor_sems, own_sems, other_sems = refs
        loads = first_loads(
            where, rows, (left_hbm, left_dir_hbm), (left, left_dir), factor_sems,
            (ratings, mask), (own_ratings, own_mask), own_sems,
        )
        late = other_loads(
            where, range(1, ratings.shape[1] // 128), pl.ds(0, mask.shape[0]),
            (ratings, mask), (all_ratings, all_mask), other_sems,
        )
        for copy in itertools.chain(*loads):
            copy.start()
    rank2, wide = panels[0].shape
    rank = rank2 // 2
    half = rank // 2
    flip = where[ratings.shape[1] // wide if first else blocks] == 1

    def own_first(x):
        return jnp.where(flip, jnp.concatenate([x[half:], x[:half]], axis=0), x)

    for k in range(blocks):
        p, d = panels[k][:rank], panels[k][rank:]
        zero = jnp.zeros_like(p)
        q = jnp.concatenate([jnp.concatenate([p, d], axis=1), jnp.concatenate([zero, p], axis=1)], axis=0)
        high, low = halves(q)
        forward[k, : 2 * rank] = high
        forward[k, 2 * rank :] = high
        forward_low[k] = low
        p, d, zero = own_first(p), own_first(d), zero[:half]
        s = jnp.concatenate(
            [
                jnp.concatenate([p[:half], zero], axis=1),
                jnp.concatenate([d[:half], p[:half]], axis=1),
                jnp.concatenate([p[half:], zero], axis=1),
                jnp.concatenate([d[half:], p[half:]], axis=1),
            ],
            axis=0,
        ).T
        high, low = halves(s)
        back[k, :, : 2 * rank] = high
        back[k, :, 2 * rank :] = low
        items[k][...] = jnp.zeros_like(items[k])
    curve[...] = jnp.zeros_like(curve)

    def do(step):
        here = pl.ds(step, rows)
        if first:
            for copy in loads[step // rows]:
                copy.wait()
            if step == start:
                for copy in late:
                    copy.start()
            both = jnp.concatenate([left[:, here], left_dir[:, here]], axis=0)
            high, low = halves(both)
            factors[: 2 * rank, here] = high
            factors[2 * rank :, here] = low
            high_t, low_t = halves(both.T)
            factors_t[here, : 2 * rank] = high_t
            factors_t[here, 2 * rank :] = low_t
            total = None
        else:
            total = acc[here, :]
        for k in range(blocks):
            if first:
                rating, seen = own_ratings[here, :], own_mask[here, :]
            else:
                columns = pl.ds(pl.multiple_of(where[k] * wide, wide), wide)
                rating, seen = ratings[here, columns], mask[here, columns]
            seen = seen.astype(F32)
            raw = dot(factors_t[here, :], forward[k]) + dot(factors_t[here, : 2 * rank], forward_low[k])
            seen = jnp.concatenate(
                [
                    seen[t * tile : (t + 1) * tile]
                    * (pattern[where[k], step // tile + t].astype(F32) * (1.0 / 64.0))
                    for t in range(rows // tile)
                ],
                axis=0,
            )
            res = seen * (raw[:, :wide] - rating)
            change = seen * raw[:, wide:]
            rc_high, rc_low = halves(jnp.concatenate([res, change], axis=1))
            out = dot(rc_high, back[k])
            out = out[:, : 2 * rank] + out[:, 2 * rank :] + dot(rc_low, back[k, :, : 2 * rank])
            total = out if total is None else total + out
            got = dot(factors[:, here], rc_high)
            got = got[: 2 * rank] + got[2 * rank :] + dot(factors[: 2 * rank, here], rc_low)
            items[k][:rank] += got[:rank, :wide]
            items[k][rank:] += got[:rank, wide:] + got[rank:, :wide]
        if last:
            user = total.T
            there = pl.ds(step - start, rows)
            keep[:, there] = user[:rank]
            send[:, there] = user[rank:]
            turned = own_first(left_dir[:, here])
            curve[...] += tile_sum(turned[:half] * user[half:rank] + turned[half:] * user[rank + half :])
        else:
            acc_out[here, :] = total

    for s in range(start, stop, rows):
        do(s)
    if first:
        for copy in late:
            copy.wait()
    for k in range(blocks):
        curve[...] += tile_sum(items[k][rank:] * panels[k][rank:])


def block_call(where, pattern, ratings, mask, given, panels, first=False, last=False, span=None, rows=512, name="block"):
    users, width = ratings.shape
    rank = panels[0].shape[0] // 2
    wide = panels[0].shape[1]
    blocks = len(panels)
    span = span or (0, users)
    count = span[1] - span[0]
    shape = jax.ShapeDtypeStruct
    outs = []
    scratch = [
        pltpu.VMEM((blocks, 4 * rank, 2 * wide), BF16),
        pltpu.VMEM((blocks, 2 * rank, 2 * wide), BF16),
        pltpu.VMEM((blocks, 2 * wide, 4 * rank), BF16),
    ]
    if first:
        outs += [shape((users, 4 * rank), BF16), shape((4 * rank, users), BF16)]
        outs += [shape(x.shape, x.dtype) for x in (ratings, mask, given[1])]
        steps = users // rows
        scratch += [
            pltpu.VMEM((rank, users), F32),
            pltpu.VMEM((users, wide), ratings.dtype),
            pltpu.VMEM((users, wide), mask.dtype),
            pltpu.SemaphoreType.DMA((2, steps)),
            pltpu.SemaphoreType.DMA((2, steps)),
            pltpu.SemaphoreType.DMA((2, width // wide - 1)),
        ]
    outs += [shape((rank, count), F32)] * 2 if last else [shape((users, 2 * rank), F32)]
    outs += [shape((1, 128), F32)] + [shape((2 * rank, wide), F32)] * blocks
    args = [ratings, mask, *given, *panels]
    far = 4 if first else 0
    args = [pltpu.with_memory_space_constraint(a, pltpu.HBM) for a in args[:far]] + [pltpu.with_memory_space_constraint(a, pltpu.VMEM) for a in args[far:]]
    return pl.pallas_call(
        functools.partial(block_kernel, blocks, first, last, span, rows, users // pattern.shape[1]),
        in_specs=[SMEM, SMEM] + [HBM] * far + [VMEM] * (len(args) - far),
        out_specs=[VMEM] * len(outs),
        out_shape=outs,
        scratch_shapes=scratch,
        compiler_params=pltpu.CompilerParams(vmem_limit_bytes=24 * 1024 * 1024),
        cost_estimate=pl.CostEstimate(flops=2 * count * wide * blocks * rank * 54, bytes_accessed=8 * count * wide * blocks, transcendentals=0),
        name=name,
    )(where, pltpu.with_memory_space_constraint(pattern, pltpu.HBM), *args)


def items_kernel(count, curves, *refs):
    terms, curve, (grad, hess, sums) = refs[:count], refs[count : count + curves], refs[count + curves :]
    total = functools.reduce(jnp.add, [t[...] for t in terms])
    rank = total.shape[0] // 2
    grad[...] = total[:rank]
    hess[...] = total[rank:]
    squares = jnp.sum(total[:rank] * total[:rank], axis=0, keepdims=True)
    wide = squares.shape[1]
    if wide < 128:
        squares = jnp.concatenate([squares, jnp.zeros((1, 128 - wide), F32)], axis=1)
    curve = functools.reduce(jnp.add, [c[...] for c in curve])
    sums[...] = jnp.concatenate([squares, curve, jnp.zeros((6, 128), F32)], axis=0)


def small_call(kernel, args, outs, name):
    args = [pltpu.with_memory_space_constraint(a, pltpu.VMEM) for a in args]
    return pl.pallas_call(
        kernel,
        in_specs=[VMEM] * len(args),
        out_specs=[VMEM] * len(outs),
        out_shape=[jax.ShapeDtypeStruct(o, F32) for o in outs],
        compiler_params=pltpu.CompilerParams(vmem_limit_bytes=4 * 1024 * 1024),
        name=name,
    )(*args)


def items_call(terms, curves):
    return small_call(
        functools.partial(items_kernel, len(terms), len(curves)),
        [*terms, *curves],
        [(terms[0].shape[0] // 2, terms[0].shape[1])] * 2 + [(8, 128)],
        "items_total",
    )


def squares_kernel(copies, a, b, sums, total, new):
    x = a[...] + b[...]
    total[...] = x
    new[...] = sums[...]
    new[0:1] += tile_sum(x * x) * (1.0 / copies)


def squares_call(a, b, sums, copies):
    return small_call(functools.partial(squares_kernel, copies), [a, b, sums], [a.shape, sums.shape], "squares")


def add_kernel(a, b, after, total):
    total[...] = a[...] + b[...]


def add_call(a, b, after):
    return small_call(add_kernel, [a, b, after], [a.shape], "add")[0]


def inner_kernel(a, b, g, h, inner):
    x = a[...] + b[...]
    inner[0] = jnp.sum(x[0:1])
    inner[1] = jnp.sum(x[1:2])


def inner_call(a, b, g, h):
    a, b = (pltpu.with_memory_space_constraint(x, pltpu.VMEM) for x in (a, b))
    return pl.pallas_call(
        inner_kernel,
        in_specs=[VMEM, VMEM, HBM, HBM],
        out_specs=SMEM,
        out_shape=jax.ShapeDtypeStruct((2,), F32),
        compiler_params=pltpu.CompilerParams(vmem_limit_bytes=4 * 1024 * 1024),
        name="inner",
    )(a, b, g, h)


def swap(x, axis, bit):
    return lax.ppermute(x, axis, [(i, i ^ bit) for i in range(lax.axis_size(axis))])


def swap_both(x, users_bit, items_bit):
    users, items = lax.axis_size("users"), lax.axis_size("items")
    pairs = [(u * items + i, (u ^ users_bit) * items + (i ^ items_bit)) for u in range(users) for i in range(items)]
    return lax.ppermute(x, ("users", "items"), pairs)


def bits(axis):
    return [1 << i for i in range(lax.axis_size(axis).bit_length() - 1)]


def per_device(ratings, entry_mask, pattern, left, left_dir, right, right_dir):
    rank = left.shape[1]
    wide = right.shape[0]
    n = lax.axis_size("users")
    me = lax.axis_index("users")
    core = lax.axis_index("items") % 2
    own = jnp.concatenate([right.T, right_dir.T], axis=0)
    direct = wide == 128
    if direct:
        panels = [own] + [swap(own, "users", k) for k in range(1, n)]
        index = [me ^ k for k in range(n)]
    else:
        panel = lax.all_gather(own, "users", axis=1, tiled=True)
        panels = [panel[:, i : i + 128] for i in range(0, panel.shape[1], 128)]
        index = list(range(len(panels)))

    def where(blocks):
        return jnp.stack([jnp.asarray(i, jnp.int32) for i in [index[k] for k in blocks] + [core]])

    table = pattern.T
    factors_t, factors, ratings, entry_mask, left_dir_t, acc, curve_a, item = block_call(
        where(range(len(panels))), table, ratings, entry_mask, [left.T, left_dir.T], panels[:1],
        first=True, rows=1024, name="own_block",
    )
    others = list(range(1, len(panels)))
    keep, send, curve_b, *rest = block_call(
        where(others), table, ratings, entry_mask, [factors_t, factors, acc, left_dir_t], panels[1:],
        last=True, rows=1024, name="other_blocks",
    )
    items = [item, *rest]
    got = swap(send, "items", 1)
    half = rank // 2
    g = keep[:half] + got[:half]
    h = keep[half:] + got[half:]
    across = bits("items")[1:]
    for bit in across[:-1]:
        g = g + swap(g, "items", bit)
        h = h + swap(h, "items", bit)
    other_g = swap(g, "items", across[-1])
    other_h = swap(h, "items", across[-1])
    if direct:
        terms = [items[0]] + [swap(items[k], "users", k) for k in range(n - 1, 0, -1)]
    else:
        terms = [
            lax.psum_scatter(jnp.concatenate(items, axis=1), "users", scatter_dimension=1, tiled=True)
        ]
    grad_right, hess_right, sums = items_call(terms, [curve_a, curve_b])
    g, sums = squares_call(g, other_g, sums, lax.axis_size("items") // 2)
    h = add_call(h, other_h, sums)
    for bit in across[:-1]:
        sums = sums + swap(sums, "items", bit)
    sums = (sums + swap(sums, "users", 1)) + (swap(sums, "items", across[-1]) + swap_both(sums, 1, across[-1]))
    for bit in bits("users")[1:]:
        sums = sums + swap(sums, "users", bit)
    far = swap(sums, "items", 1)

    def joined(mine):
        other = swap(mine, "items", 1)
        return jnp.concatenate([jnp.where(core == 0, mine, other), jnp.where(core == 0, other, mine)], axis=0)

    g, h = joined(g), joined(h)
    inner = inner_call(sums, far, g, h)
    return g.T, h.T, grad_right.T, hess_right.T, inner


def solution(mesh):
    placed = (
        P(("copies", "users"), "items"),
        P(("copies", "users"), "items"),
        P(("copies", "users"), "items"),
        P(("copies", "users"), None),
        P(("copies", "users"), None),
        P(("copies", "items", "users"), None),
        P(("copies", "items", "users"), None),
    )
    return jax.shard_map(
        per_device,
        mesh=mesh,
        in_specs=placed,
        out_specs=(
            P(("copies", "users"), None),
            P(("copies", "users"), None),
            P(("copies", "items", "users"), None),
            P(("copies", "items", "users"), None),
            P("copies"),
        ),
        check_vma=False,
    )
```

```python
import functools
import itertools
import jax
import jax.numpy as jnp
from jax import lax
from jax.experimental import pallas as pl
from jax.experimental.pallas import tpu as pltpu
from jax.sharding import PartitionSpec as P

F32 = jnp.float32
BF16 = jnp.bfloat16
HEAVY = 20_000_000_000
SMEM = pl.BlockSpec(memory_space=pltpu.SMEM)
VMEM = pl.BlockSpec(memory_space=pltpu.VMEM)
HBM = pl.BlockSpec(memory_space=pltpu.HBM)


def dot(a, b):
    return jnp.dot(a, b, preferred_element_type=F32)


def halves(x):
    high = x.astype(BF16)
    return high, (x - high.astype(F32)).astype(BF16)


def tile_sum(x):
    total = jnp.sum(x, axis=0, keepdims=True)
    return functools.reduce(jnp.add, [total[:, i : i + 128] for i in range(0, total.shape[1], 128)])


def first_loads(where, rows, factors, factors_to, factor_sems, grids, grids_to, own_sems):
    users, width = grids[0].shape
    wide = 128
    block = lambda k: pl.ds(pl.multiple_of(where[k] * wide, wide), wide)
    steps = []
    for step in range(users // rows):
        here = pl.ds(step * rows, rows)
        steps.append(
            [
                pltpu.make_async_copy(a.at[:, here], b.at[:, here], factor_sems.at[i, step])
                for i, (a, b) in enumerate(zip(factors, factors_to))
            ]
            + [
                pltpu.make_async_copy(a.at[here, block(0)], b.at[here], own_sems.at[i, step])
                for i, (a, b) in enumerate(zip(grids, grids_to))
            ]
        )
    return steps


def other_loads(where, blocks, here, grids, grids_to, sems):
    wide = 128
    block = lambda k: pl.ds(pl.multiple_of(where[k] * wide, wide), wide)
    return [
        pltpu.make_async_copy(a.at[here, block(k)], b.at[:, block(k)], sems.at[i, j])
        for j, k in enumerate(blocks)
        for i, (a, b) in enumerate(zip(grids, grids_to))
    ]


def block_kernel(blocks, first, last, span, rows, tile, where, pattern, ratings, mask, *refs):
    refs = list(refs)
    take = lambda n: [refs.pop(0) for _ in range(n)]
    if first:
        left_hbm, left_dir_hbm = take(2)
    else:
        factors_t, factors, acc = take(3)
        left_dir = take(1)[0] if last else None
    panels = take(blocks)
    start, stop = span
    if first:
        factors_t, factors, all_ratings, all_mask, left_dir = take(5)
    if last:
        keep, send = take(2)
    else:
        acc_out = take(1)[0]
    curve = take(1)[0]
    items = take(blocks)
    forward, forward_low, back = take(3)
    if first:
        left, own_ratings, own_mask, factor_sems, own_sems, other_sems = refs
        loads = first_loads(
            where, rows, (left_hbm, left_dir_hbm), (left, left_dir), factor_sems,
            (ratings, mask), (own_ratings, own_mask), own_sems,
        )
        late = other_loads(
            where, range(1, ratings.shape[1] // 128), pl.ds(0, mask.shape[0]),
            (ratings, mask), (all_ratings, all_mask), other_sems,
        )
        for copy in itertools.chain(*loads):
            copy.start()
    rank2, wide = panels[0].shape
    rank = rank2 // 2
    half = rank // 2
    flip = where[ratings.shape[1] // wide if first else blocks] == 1

    def own_first(x):
        return jnp.where(flip, jnp.concatenate([x[half:], x[:half]], axis=0), x)

    for k in range(blocks):
        p, d = panels[k][:rank], panels[k][rank:]
        zero = jnp.zeros_like(p)
        q = jnp.concatenate([jnp.concatenate([p, d], axis=1), jnp.concatenate([zero, p], axis=1)], axis=0)
        high, low = halves(q)
        forward[k, : 2 * rank] = high
        forward[k, 2 * rank :] = high
        forward_low[k] = low
        p, d, zero = own_first(p), own_first(d), zero[:half]
        s = jnp.concatenate(
            [
                jnp.concatenate([p[:half], zero], axis=1),
                jnp.concatenate([d[:half], p[:half]], axis=1),
                jnp.concatenate([p[half:], zero], axis=1),
                jnp.concatenate([d[half:], p[half:]], axis=1),
            ],
            axis=0,
        ).T
        high, low = halves(s)
        back[k, :, : 2 * rank] = high
        back[k, :, 2 * rank :] = low
        items[k][...] = jnp.zeros_like(items[k])
    curve[...] = jnp.zeros_like(curve)

    def do(step):
        here = pl.ds(step, rows)
        if first:
            for copy in loads[step // rows]:
                copy.wait()
            if step == start:
                for copy in late:
                    copy.start()
            both = jnp.concatenate([left[:, here], left_dir[:, here]], axis=0)
            high, low = halves(both)
            factors[: 2 * rank, here] = high
            factors[2 * rank :, here] = low
            high_t, low_t = halves(both.T)
            factors_t[here, : 2 * rank] = high_t
            factors_t[here, 2 * rank :] = low_t
            total = None
        else:
            total = acc[here, :]
        for k in range(blocks):
            if first:
                rating, seen = own_ratings[here, :], own_mask[here, :]
            else:
                columns = pl.ds(pl.multiple_of(where[k] * wide, wide), wide)
                rating, seen = ratings[here, columns], mask[here, columns]
            seen = seen.astype(F32)
            raw = dot(factors_t[here, :], forward[k]) + dot(factors_t[here, : 2 * rank], forward_low[k])
            seen = jnp.concatenate(
                [
                    seen[t * tile : (t + 1) * tile]
                    * (pattern[where[k], step // tile + t].astype(F32) * (1.0 / 64.0))
                    for t in range(rows // tile)
                ],
                axis=0,
            )
            res = seen * (raw[:, :wide] - rating)
            change = seen * raw[:, wide:]
            rc_high, rc_low = halves(jnp.concatenate([res, change], axis=1))
            out = dot(rc_high, back[k])
            out = out[:, : 2 * rank] + out[:, 2 * rank :] + dot(rc_low, back[k, :, : 2 * rank])
            total = out if total is None else total + out
            got = dot(factors[:, here], rc_high)
            got = got[: 2 * rank] + got[2 * rank :] + dot(factors[: 2 * rank, here], rc_low)
            items[k][:rank] += got[:rank, :wide]
            items[k][rank:] += got[:rank, wide:] + got[rank:, :wide]
        if last:
            user = total.T
            there = pl.ds(step - start, rows)
            keep[:, there] = user[:rank]
            send[:, there] = user[rank:]
            turned = own_first(left_dir[:, here])
            curve[...] += tile_sum(turned[:half] * user[half:rank] + turned[half:] * user[rank + half :])
        else:
            acc_out[here, :] = total

    for s in range(start, stop, rows):
        do(s)
    if first:
        for copy in late:
            copy.wait()
    for k in range(blocks):
        curve[...] += tile_sum(items[k][rank:] * panels[k][rank:])


def block_call(where, pattern, ratings, mask, given, panels, first=False, last=False, span=None, rows=512, name="block"):
    users, width = ratings.shape
    rank = panels[0].shape[0] // 2
    wide = panels[0].shape[1]
    blocks = len(panels)
    span = span or (0, users)
    count = span[1] - span[0]
    shape = jax.ShapeDtypeStruct
    outs = []
    scratch = [
        pltpu.VMEM((blocks, 4 * rank, 2 * wide), BF16),
        pltpu.VMEM((blocks, 2 * rank, 2 * wide), BF16),
        pltpu.VMEM((blocks, 2 * wide, 4 * rank), BF16),
    ]
    if first:
        outs += [shape((users, 4 * rank), BF16), shape((4 * rank, users), BF16)]
        outs += [shape(x.shape, x.dtype) for x in (ratings, mask, given[1])]
        steps = users // rows
        scratch += [
            pltpu.VMEM((rank, users), F32),
            pltpu.VMEM((users, wide), ratings.dtype),
            pltpu.VMEM((users, wide), mask.dtype),
            pltpu.SemaphoreType.DMA((2, steps)),
            pltpu.SemaphoreType.DMA((2, steps)),
            pltpu.SemaphoreType.DMA((2, width // wide - 1)),
        ]
    outs += [shape((rank, count), F32)] * 2 if last else [shape((users, 2 * rank), F32)]
    outs += [shape((1, 128), F32)] + [shape((2 * rank, wide), F32)] * blocks
    args = [ratings, mask, *given, *panels]
    far = 4 if first else 0
    args = [pltpu.with_memory_space_constraint(a, pltpu.HBM) for a in args[:far]] + [pltpu.with_memory_space_constraint(a, pltpu.VMEM) for a in args[far:]]
    return pl.pallas_call(
        functools.partial(block_kernel, blocks, first, last, span, rows, users // pattern.shape[1]),
        in_specs=[SMEM, SMEM] + [HBM] * far + [VMEM] * (len(args) - far),
        out_specs=[VMEM] * len(outs),
        out_shape=outs,
        scratch_shapes=scratch,
        compiler_params=pltpu.CompilerParams(vmem_limit_bytes=24 * 1024 * 1024),
        cost_estimate=pl.CostEstimate(flops=2 * count * wide * blocks * rank * 54, bytes_accessed=8 * count * wide * blocks, transcendentals=0),
        name=name,
    )(where, pltpu.with_memory_space_constraint(pattern, pltpu.HBM), *args)


def items_kernel(count, curves, *refs):
    terms, curve, (grad, hess, sums) = refs[:count], refs[count : count + curves], refs[count + curves :]
    total = functools.reduce(jnp.add, [t[...] for t in terms])
    rank = total.shape[0] // 2
    grad[...] = total[:rank]
    hess[...] = total[rank:]
    squares = jnp.sum(total[:rank] * total[:rank], axis=0, keepdims=True)
    wide = squares.shape[1]
    if wide < 128:
        squares = jnp.concatenate([squares, jnp.zeros((1, 128 - wide), F32)], axis=1)
    curve = functools.reduce(jnp.add, [c[...] for c in curve])
    sums[...] = jnp.concatenate([squares, curve, jnp.zeros((6, 128), F32)], axis=0)


def small_call(kernel, args, outs, name, flops=0):
    args = [pltpu.with_memory_space_constraint(a, pltpu.VMEM) for a in args]
    return pl.pallas_call(
        kernel,
        in_specs=[VMEM] * len(args),
        out_specs=[VMEM] * len(outs),
        out_shape=[jax.ShapeDtypeStruct(o, F32) for o in outs],
        compiler_params=pltpu.CompilerParams(vmem_limit_bytes=4 * 1024 * 1024),
        cost_estimate=pl.CostEstimate(flops=flops, bytes_accessed=0, transcendentals=0),
        name=name,
    )(*args)


def items_call(terms, curves):
    return small_call(
        functools.partial(items_kernel, len(terms), len(curves)),
        [*terms, *curves],
        [(terms[0].shape[0] // 2, terms[0].shape[1])] * 2 + [(8, 128)],
        "items_total",
        HEAVY,
    )


def squares_kernel(copies, a, b, sums, total, new):
    x = a[...] + b[...]
    total[...] = x
    new[...] = sums[...]
    new[0:1] += tile_sum(x * x) * (1.0 / copies)


def squares_call(a, b, sums, copies):
    return small_call(functools.partial(squares_kernel, copies), [a, b, sums], [a.shape, sums.shape], "squares")


def add_kernel(a, b, after, total):
    total[...] = a[...] + b[...]


def add_call(a, b, after):
    return small_call(add_kernel, [a, b, after], [a.shape], "add")[0]


def inner_kernel(a, b, g, h, inner):
    x = a[...] + b[...]
    inner[0] = jnp.sum(x[0:1])
    inner[1] = jnp.sum(x[1:2])


def inner_call(a, b, g, h):
    a, b = (pltpu.with_memory_space_constraint(x, pltpu.VMEM) for x in (a, b))
    return pl.pallas_call(
        inner_kernel,
        in_specs=[VMEM, VMEM, HBM, HBM],
        out_specs=SMEM,
        out_shape=jax.ShapeDtypeStruct((2,), F32),
        compiler_params=pltpu.CompilerParams(vmem_limit_bytes=4 * 1024 * 1024),
        name="inner",
    )(a, b, g, h)


def swap(x, axis, bit):
    return lax.ppermute(x, axis, [(i, i ^ bit) for i in range(lax.axis_size(axis))])


def swap_both(x, users_bit, items_bit):
    users, items = lax.axis_size("users"), lax.axis_size("items")
    pairs = [(u * items + i, (u ^ users_bit) * items + (i ^ items_bit)) for u in range(users) for i in range(items)]
    return lax.ppermute(x, ("users", "items"), pairs)


def bits(axis):
    return [1 << i for i in range(lax.axis_size(axis).bit_length() - 1)]


def per_device(ratings, entry_mask, pattern, left, left_dir, right, right_dir):
    rank = left.shape[1]
    wide = right.shape[0]
    n = lax.axis_size("users")
    me = lax.axis_index("users")
    core = lax.axis_index("items") % 2
    own = jnp.concatenate([right.T, right_dir.T], axis=0)
    direct = wide == 128
    if direct:
        panels = [own] + [swap(own, "users", k) for k in range(1, n)]
        index = [me ^ k for k in range(n)]
    else:
        panel = lax.all_gather(own, "users", axis=1, tiled=True)
        panels = [panel[:, i : i + 128] for i in range(0, panel.shape[1], 128)]
        index = list(range(len(panels)))

    def where(blocks):
        return jnp.stack([jnp.asarray(i, jnp.int32) for i in [index[k] for k in blocks] + [core]])

    table = pattern.T
    factors_t, factors, ratings, entry_mask, left_dir_t, acc, curve_a, item = block_call(
        where(range(len(panels))), table, ratings, entry_mask, [left.T, left_dir.T], panels[:1],
        first=True, rows=1024, name="own_block",
    )
    others = list(range(1, len(panels)))
    keep, send, curve_b, *rest = block_call(
        where(others), table, ratings, entry_mask, [factors_t, factors, acc, left_dir_t], panels[1:],
        last=True, rows=1024, name="other_blocks",
    )
    items = [item, *rest]
    got = swap(send, "items", 1)
    half = rank // 2
    g = keep[:half] + got[:half]
    h = keep[half:] + got[half:]
    across = bits("items")[1:]
    for bit in across[:-1]:
        g = g + swap(g, "items", bit)
        h = h + swap(h, "items", bit)
    other_g = swap(g, "items", across[-1])
    other_h = swap(h, "items", across[-1])
    if direct:
        terms = [items[0]] + [swap(items[k], "users", k) for k in range(n - 1, 0, -1)]
    else:
        terms = [
            lax.psum_scatter(jnp.concatenate(items, axis=1), "users", scatter_dimension=1, tiled=True)
        ]
    grad_right, hess_right, sums = items_call(terms, [curve_a, curve_b])
    for bit in across:
        sums = sums + swap(sums, "items", bit)
    g, sums = squares_call(g, other_g, sums, 1)
    h = add_call(h, other_h, sums)
    for bit in bits("users"):
        sums = sums + swap(sums, "users", bit)
    far = swap(sums, "items", 1)

    def joined(mine):
        other = swap(mine, "items", 1)
        return jnp.concatenate([jnp.where(core == 0, mine, other), jnp.where(core == 0, other, mine)], axis=0)

    g, h = joined(g), joined(h)
    inner = inner_call(sums, far, g, h)
    return g.T, h.T, grad_right.T, hess_right.T, inner


def solution(mesh):
    placed = (
        P(("copies", "users"), "items"),
        P(("copies", "users"), "items"),
        P(("copies", "users"), "items"),
        P(("copies", "users"), None),
        P(("copies", "users"), None),
        P(("copies", "items", "users"), None),
        P(("copies", "items", "users"), None),
    )
    return jax.shard_map(
        per_device,
        mesh=mesh,
        in_specs=placed,
        out_specs=(
            P(("copies", "users"), None),
            P(("copies", "users"), None),
            P(("copies", "items", "users"), None),
            P(("copies", "items", "users"), None),
            P("copies"),
        ),
        check_vma=False,
    )
```

```python
import functools
import itertools
import jax
import jax.numpy as jnp
from jax import lax
from jax.experimental import pallas as pl
from jax.experimental.pallas import tpu as pltpu
from jax.sharding import PartitionSpec as P

F32 = jnp.float32
BF16 = jnp.bfloat16
HEAVY = 20_000_000_000
SMEM = pl.BlockSpec(memory_space=pltpu.SMEM)
VMEM = pl.BlockSpec(memory_space=pltpu.VMEM)
HBM = pl.BlockSpec(memory_space=pltpu.HBM)


def dot(a, b):
    return jnp.dot(a, b, preferred_element_type=F32)


def halves(x):
    high = x.astype(BF16)
    return high, (x - high.astype(F32)).astype(BF16)


def tile_sum(x):
    total = jnp.sum(x, axis=0, keepdims=True)
    return functools.reduce(jnp.add, [total[:, i : i + 128] for i in range(0, total.shape[1], 128)])


def first_loads(where, rows, factors, factors_to, factor_sems, grids, grids_to, own_sems):
    users, width = grids[0].shape
    wide = 128
    block = lambda k: pl.ds(pl.multiple_of(where[k] * wide, wide), wide)
    steps = []
    for step in range(users // rows):
        here = pl.ds(step * rows, rows)
        steps.append(
            [
                pltpu.make_async_copy(a.at[:, here], b.at[:, here], factor_sems.at[i, step])
                for i, (a, b) in enumerate(zip(factors, factors_to))
            ]
            + [
                pltpu.make_async_copy(a.at[here, block(0)], b.at[here], own_sems.at[i, step])
                for i, (a, b) in enumerate(zip(grids, grids_to))
            ]
        )
    return steps


def other_loads(where, blocks, here, grids, grids_to, sems):
    wide = 128
    block = lambda k: pl.ds(pl.multiple_of(where[k] * wide, wide), wide)
    return [
        pltpu.make_async_copy(a.at[here, block(k)], b.at[:, block(k)], sems.at[i, j])
        for j, k in enumerate(blocks)
        for i, (a, b) in enumerate(zip(grids, grids_to))
    ]


def block_kernel(blocks, first, last, span, rows, tile, where, pattern, ratings, mask, *refs):
    refs = list(refs)
    take = lambda n: [refs.pop(0) for _ in range(n)]
    if first:
        left_hbm, left_dir_hbm = take(2)
    else:
        factors_t, factors, acc = take(3)
        left_dir = take(1)[0] if last else None
    panels = take(blocks)
    start, stop = span
    if first:
        factors_t, factors, all_ratings, all_mask, left_dir = take(5)
    if last:
        keep, send = take(2)
    else:
        acc_out = take(1)[0]
    curve = take(1)[0]
    items = take(blocks)
    forward, forward_low, back = take(3)
    if first:
        left, own_ratings, own_mask, factor_sems, own_sems, other_sems = refs
        loads = first_loads(
            where, rows, (left_hbm, left_dir_hbm), (left, left_dir), factor_sems,
            (ratings, mask), (own_ratings, own_mask), own_sems,
        )
        late = other_loads(
            where, range(1, ratings.shape[1] // 128), pl.ds(0, mask.shape[0]),
            (ratings, mask), (all_ratings, all_mask), other_sems,
        )
        for copy in itertools.chain(*loads):
            copy.start()
    rank2, wide = panels[0].shape
    rank = rank2 // 2
    half = rank // 2
    flip = where[ratings.shape[1] // wide if first else blocks] == 1

    def own_first(x):
        return jnp.where(flip, jnp.concatenate([x[half:], x[:half]], axis=0), x)

    for k in range(blocks):
        p, d = panels[k][:rank], panels[k][rank:]
        zero = jnp.zeros_like(p)
        q = jnp.concatenate([jnp.concatenate([p, d], axis=1), jnp.concatenate([zero, p], axis=1)], axis=0)
        high, low = halves(q)
        forward[k, : 2 * rank] = high
        forward[k, 2 * rank :] = high
        forward_low[k] = low
        p, d, zero = own_first(p), own_first(d), zero[:half]
        s = jnp.concatenate(
            [
                jnp.concatenate([p[:half], zero], axis=1),
                jnp.concatenate([d[:half], p[:half]], axis=1),
                jnp.concatenate([p[half:], zero], axis=1),
                jnp.concatenate([d[half:], p[half:]], axis=1),
            ],
            axis=0,
        ).T
        high, low = halves(s)
        back[k, :, : 2 * rank] = high
        back[k, :, 2 * rank :] = low
        items[k][...] = jnp.zeros_like(items[k])
    curve[...] = jnp.zeros_like(curve)

    def do(step):
        here = pl.ds(step, rows)
        if first:
            for copy in loads[step // rows]:
                copy.wait()
            if step == start:
                for copy in late:
                    copy.start()
            both = jnp.concatenate([left[:, here], left_dir[:, here]], axis=0)
            high, low = halves(both)
            factors[: 2 * rank, here] = high
            factors[2 * rank :, here] = low
            high_t, low_t = halves(both.T)
            factors_t[here, : 2 * rank] = high_t
            factors_t[here, 2 * rank :] = low_t
            total = None
        else:
            total = acc[here, :]
        highs, lows = [], []
        for k in range(blocks):
            if first:
                rating, seen = own_ratings[here, :], own_mask[here, :]
            else:
                columns = pl.ds(pl.multiple_of(where[k] * wide, wide), wide)
                rating, seen = ratings[here, columns], mask[here, columns]
            seen = seen.astype(F32)
            raw = dot(factors_t[here, :], forward[k]) + dot(factors_t[here, : 2 * rank], forward_low[k])
            seen = jnp.concatenate(
                [
                    seen[t * tile : (t + 1) * tile]
                    * (pattern[where[k], step // tile + t].astype(F32) * (1.0 / 64.0))
                    for t in range(rows // tile)
                ],
                axis=0,
            )
            res = seen * (raw[:, :wide] - rating)
            change = seen * raw[:, wide:]
            rc_high, rc_low = halves(jnp.concatenate([res, change], axis=1))
            out = dot(rc_high, back[k])
            out = out[:, : 2 * rank] + out[:, 2 * rank :] + dot(rc_low, back[k, :, : 2 * rank])
            total = out if total is None else total + out
            highs.append(rc_high)
            lows.append(rc_low)
        f = factors[:, here]
        got = dot(f, jnp.concatenate(highs, axis=1))
        got = got[: 2 * rank] + got[2 * rank :] + dot(f[: 2 * rank], jnp.concatenate(lows, axis=1))
        for k in range(blocks):
            items[k][:rank] += got[:rank, 2 * k * wide : (2 * k + 1) * wide]
            items[k][rank:] += got[:rank, (2 * k + 1) * wide : (2 * k + 2) * wide] + got[rank:, 2 * k * wide : (2 * k + 1) * wide]
        if last:
            user = total.T
            there = pl.ds(step - start, rows)
            keep[:, there] = user[:rank]
            send[:, there] = user[rank:]
            turned = own_first(left_dir[:, here])
            curve[...] += tile_sum(turned[:half] * user[half:rank] + turned[half:] * user[rank + half :])
        else:
            acc_out[here, :] = total

    for s in range(start, stop, rows):
        do(s)
    if first:
        for copy in late:
            copy.wait()
    for k in range(blocks):
        curve[...] += tile_sum(items[k][rank:] * panels[k][rank:])


def block_call(where, pattern, ratings, mask, given, panels, first=False, last=False, span=None, rows=512, name="block"):
    users, width = ratings.shape
    rank = panels[0].shape[0] // 2
    wide = panels[0].shape[1]
    blocks = len(panels)
    span = span or (0, users)
    count = span[1] - span[0]
    shape = jax.ShapeDtypeStruct
    outs = []
    scratch = [
        pltpu.VMEM((blocks, 4 * rank, 2 * wide), BF16),
        pltpu.VMEM((blocks, 2 * rank, 2 * wide), BF16),
        pltpu.VMEM((blocks, 2 * wide, 4 * rank), BF16),
    ]
    if first:
        outs += [shape((users, 4 * rank), BF16), shape((4 * rank, users), BF16)]
        outs += [shape(x.shape, x.dtype) for x in (ratings, mask, given[1])]
        steps = users // rows
        scratch += [
            pltpu.VMEM((rank, users), F32),
            pltpu.VMEM((users, wide), ratings.dtype),
            pltpu.VMEM((users, wide), mask.dtype),
            pltpu.SemaphoreType.DMA((2, steps)),
            pltpu.SemaphoreType.DMA((2, steps)),
            pltpu.SemaphoreType.DMA((2, width // wide - 1)),
        ]
    outs += [shape((rank, count), F32)] * 2 if last else [shape((users, 2 * rank), F32)]
    outs += [shape((1, 128), F32)] + [shape((2 * rank, wide), F32)] * blocks
    args = [ratings, mask, *given, *panels]
    far = 4 if first else 0
    args = [pltpu.with_memory_space_constraint(a, pltpu.HBM) for a in args[:far]] + [pltpu.with_memory_space_constraint(a, pltpu.VMEM) for a in args[far:]]
    return pl.pallas_call(
        functools.partial(block_kernel, blocks, first, last, span, rows, users // pattern.shape[1]),
        in_specs=[SMEM, SMEM] + [HBM] * far + [VMEM] * (len(args) - far),
        out_specs=[VMEM] * len(outs),
        out_shape=outs,
        scratch_shapes=scratch,
        compiler_params=pltpu.CompilerParams(vmem_limit_bytes=24 * 1024 * 1024),
        cost_estimate=pl.CostEstimate(flops=2 * count * wide * blocks * rank * 54, bytes_accessed=8 * count * wide * blocks, transcendentals=0),
        name=name,
    )(where, pltpu.with_memory_space_constraint(pattern, pltpu.HBM), *args)


def items_kernel(count, curves, *refs):
    terms, curve, (grad, hess, sums) = refs[:count], refs[count : count + curves], refs[count + curves :]
    total = functools.reduce(jnp.add, [t[...] for t in terms])
    rank = total.shape[0] // 2
    grad[...] = total[:rank]
    hess[...] = total[rank:]
    squares = jnp.sum(total[:rank] * total[:rank], axis=0, keepdims=True)
    wide = squares.shape[1]
    if wide < 128:
        squares = jnp.concatenate([squares, jnp.zeros((1, 128 - wide), F32)], axis=1)
    curve = functools.reduce(jnp.add, [c[...] for c in curve])
    sums[...] = jnp.concatenate([squares, curve, jnp.zeros((6, 128), F32)], axis=0)


def small_call(kernel, args, outs, name, flops=0):
    args = [pltpu.with_memory_space_constraint(a, pltpu.VMEM) for a in args]
    return pl.pallas_call(
        kernel,
        in_specs=[VMEM] * len(args),
        out_specs=[VMEM] * len(outs),
        out_shape=[jax.ShapeDtypeStruct(o, F32) for o in outs],
        compiler_params=pltpu.CompilerParams(vmem_limit_bytes=4 * 1024 * 1024),
        cost_estimate=pl.CostEstimate(flops=flops, bytes_accessed=0, transcendentals=0),
        name=name,
    )(*args)


def items_call(terms, curves):
    return small_call(
        functools.partial(items_kernel, len(terms), len(curves)),
        [*terms, *curves],
        [(terms[0].shape[0] // 2, terms[0].shape[1])] * 2 + [(8, 128)],
        "items_total",
        HEAVY,
    )


def squares_kernel(copies, a, b, sums, total, new):
    x = a[...] + b[...]
    total[...] = x
    new[...] = sums[...]
    new[0:1] += tile_sum(x * x) * (1.0 / copies)


def squares_call(a, b, sums, copies):
    return small_call(functools.partial(squares_kernel, copies), [a, b, sums], [a.shape, sums.shape], "squares")


def add_kernel(a, b, after, total):
    total[...] = a[...] + b[...]


def add_call(a, b, after):
    return small_call(add_kernel, [a, b, after], [a.shape], "add")[0]


def inner_kernel(a, b, g, h, inner):
    x = a[...] + b[...]
    inner[0] = jnp.sum(x[0:1])
    inner[1] = jnp.sum(x[1:2])


def inner_call(a, b, g, h):
    a, b = (pltpu.with_memory_space_constraint(x, pltpu.VMEM) for x in (a, b))
    return pl.pallas_call(
        inner_kernel,
        in_specs=[VMEM, VMEM, HBM, HBM],
        out_specs=SMEM,
        out_shape=jax.ShapeDtypeStruct((2,), F32),
        compiler_params=pltpu.CompilerParams(vmem_limit_bytes=4 * 1024 * 1024),
        name="inner",
    )(a, b, g, h)


def swap(x, axis, bit):
    return lax.ppermute(x, axis, [(i, i ^ bit) for i in range(lax.axis_size(axis))])


def swap_both(x, users_bit, items_bit):
    users, items = lax.axis_size("users"), lax.axis_size("items")
    pairs = [(u * items + i, (u ^ users_bit) * items + (i ^ items_bit)) for u in range(users) for i in range(items)]
    return lax.ppermute(x, ("users", "items"), pairs)


def bits(axis):
    return [1 << i for i in range(lax.axis_size(axis).bit_length() - 1)]


def per_device(ratings, entry_mask, pattern, left, left_dir, right, right_dir):
    rank = left.shape[1]
    wide = right.shape[0]
    n = lax.axis_size("users")
    me = lax.axis_index("users")
    core = lax.axis_index("items") % 2
    own = jnp.concatenate([right.T, right_dir.T], axis=0)
    direct = wide == 128
    if direct:
        panels = [own] + [swap(own, "users", k) for k in range(1, n)]
        index = [me ^ k for k in range(n)]
    else:
        panel = lax.all_gather(own, "users", axis=1, tiled=True)
        panels = [panel[:, i : i + 128] for i in range(0, panel.shape[1], 128)]
        index = list(range(len(panels)))

    def where(blocks):
        return jnp.stack([jnp.asarray(i, jnp.int32) for i in [index[k] for k in blocks] + [core]])

    table = pattern.T
    factors_t, factors, ratings, entry_mask, left_dir_t, acc, curve_a, item = block_call(
        where(range(len(panels))), table, ratings, entry_mask, [left.T, left_dir.T], panels[:1],
        first=True, rows=1024, name="own_block",
    )
    others = list(range(1, len(panels)))
    keep, send, curve_b, *rest = block_call(
        where(others), table, ratings, entry_mask, [factors_t, factors, acc, left_dir_t], panels[1:],
        last=True, rows=2048, name="other_blocks",
    )
    items = [item, *rest]
    got = swap(send, "items", 1)
    half = rank // 2
    g = keep[:half] + got[:half]
    h = keep[half:] + got[half:]
    across = bits("items")[1:]
    for bit in across[:-1]:
        g = g + swap(g, "items", bit)
        h = h + swap(h, "items", bit)
    other_g = swap(g, "items", across[-1])
    other_h = swap(h, "items", across[-1])
    if direct:
        terms = [items[0]] + [swap(items[k], "users", k) for k in range(n - 1, 0, -1)]
    else:
        terms = [
            lax.psum_scatter(jnp.concatenate(items, axis=1), "users", scatter_dimension=1, tiled=True)
        ]
    grad_right, hess_right, sums = items_call(terms, [curve_a, curve_b])
    for bit in across:
        sums = sums + swap(sums, "items", bit)
    g, sums = squares_call(g, other_g, sums, 1)
    h = add_call(h, other_h, sums)
    for bit in bits("users"):
        sums = sums + swap(sums, "users", bit)
    far = swap(sums, "items", 1)

    def joined(mine):
        other = swap(mine, "items", 1)
        return jnp.concatenate([jnp.where(core == 0, mine, other), jnp.where(core == 0, other, mine)], axis=0)

    g, h = joined(g), joined(h)
    inner = inner_call(sums, far, g, h)
    return g.T, h.T, grad_right.T, hess_right.T, inner


def solution(mesh):
    placed = (
        P(("copies", "users"), "items"),
        P(("copies", "users"), "items"),
        P(("copies", "users"), "items"),
        P(("copies", "users"), None),
        P(("copies", "users"), None),
        P(("copies", "items", "users"), None),
        P(("copies", "items", "users"), None),
    )
    return jax.shard_map(
        per_device,
        mesh=mesh,
        in_specs=placed,
        out_specs=(
            P(("copies", "users"), None),
            P(("copies", "users"), None),
            P(("copies", "items", "users"), None),
            P(("copies", "items", "users"), None),
            P("copies"),
        ),
        check_vma=False,
    )
```

```python
import functools
import itertools
import jax
import jax.numpy as jnp
from jax import lax
from jax.experimental import pallas as pl
from jax.experimental.pallas import tpu as pltpu
from jax.sharding import PartitionSpec as P

F32 = jnp.float32
BF16 = jnp.bfloat16
HEAVY = 20_000_000_000
SMEM = pl.BlockSpec(memory_space=pltpu.SMEM)
VMEM = pl.BlockSpec(memory_space=pltpu.VMEM)
HBM = pl.BlockSpec(memory_space=pltpu.HBM)


def dot(a, b):
    return jnp.dot(a, b, preferred_element_type=F32)


def halves(x):
    high = x.astype(BF16)
    return high, (x - high.astype(F32)).astype(BF16)


def tile_sum(x):
    total = jnp.sum(x, axis=0, keepdims=True)
    return functools.reduce(jnp.add, [total[:, i : i + 128] for i in range(0, total.shape[1], 128)])


def first_loads(where, rows, factors, factors_to, factor_sems, grids, grids_to, own_sems):
    users, width = grids[0].shape
    wide = 128
    block = lambda k: pl.ds(pl.multiple_of(where[k] * wide, wide), wide)
    steps = []
    for step in range(users // rows):
        here = pl.ds(step * rows, rows)
        steps.append(
            [
                pltpu.make_async_copy(a.at[:, here], b.at[:, here], factor_sems.at[i, step])
                for i, (a, b) in enumerate(zip(factors, factors_to))
            ]
            + [
                pltpu.make_async_copy(a.at[here, block(0)], b.at[here], own_sems.at[i, step])
                for i, (a, b) in enumerate(zip(grids, grids_to))
            ]
        )
    return steps


def other_loads(where, blocks, here, grids, grids_to, sems):
    wide = 128
    block = lambda k: pl.ds(pl.multiple_of(where[k] * wide, wide), wide)
    return [
        pltpu.make_async_copy(a.at[here, block(k)], b.at[:, block(k)], sems.at[i, j])
        for j, k in enumerate(blocks)
        for i, (a, b) in enumerate(zip(grids, grids_to))
    ]


def block_kernel(blocks, first, last, span, rows, tile, where, pattern, ratings, mask, *refs):
    refs = list(refs)
    take = lambda n: [refs.pop(0) for _ in range(n)]
    if first:
        left_hbm, left_dir_hbm = take(2)
    else:
        factors_t, factors, acc = take(3)
        left_dir = take(1)[0] if last else None
    panels = take(blocks)
    start, stop = span
    if first:
        factors_t, factors, all_ratings, all_mask, left_dir = take(5)
    if last:
        keep, send = take(2)
    else:
        acc_out = take(1)[0]
    curve = take(1)[0]
    items = take(blocks)
    forward, forward_low, back = take(3)
    if first:
        left, own_ratings, own_mask, factor_sems, own_sems, other_sems = refs
        loads = first_loads(
            where, rows, (left_hbm, left_dir_hbm), (left, left_dir), factor_sems,
            (ratings, mask), (own_ratings, own_mask), own_sems,
        )
        late = other_loads(
            where, range(1, ratings.shape[1] // 128), pl.ds(0, mask.shape[0]),
            (ratings, mask), (all_ratings, all_mask), other_sems,
        )
        for copy in itertools.chain(*loads, late):
            copy.start()
    rank2, wide = panels[0].shape
    rank = rank2 // 2
    half = rank // 2
    flip = where[ratings.shape[1] // wide if first else blocks] == 1

    def own_first(x):
        return jnp.where(flip, jnp.concatenate([x[half:], x[:half]], axis=0), x)

    for k in range(blocks):
        p, d = panels[k][:rank], panels[k][rank:]
        zero = jnp.zeros_like(p)
        q = jnp.concatenate([jnp.concatenate([p, d], axis=1), jnp.concatenate([zero, p], axis=1)], axis=0)
        high, low = halves(q)
        forward[k, : 2 * rank] = high
        forward[k, 2 * rank :] = high
        forward_low[k] = low
        p, d, zero = own_first(p), own_first(d), zero[:half]
        s = jnp.concatenate(
            [
                jnp.concatenate([p[:half], zero], axis=1),
                jnp.concatenate([d[:half], p[:half]], axis=1),
                jnp.concatenate([p[half:], zero], axis=1),
                jnp.concatenate([d[half:], p[half:]], axis=1),
            ],
            axis=0,
        ).T
        high, low = halves(s)
        back[k, :, : 2 * rank] = high
        back[k, :, 2 * rank :] = low
        items[k][...] = jnp.zeros_like(items[k])
    curve[...] = jnp.zeros_like(curve)

    def do(step):
        here = pl.ds(step, rows)
        if first:
            for copy in loads[step // rows]:
                copy.wait()
            both = jnp.concatenate([left[:, here], left_dir[:, here]], axis=0)
            high, low = halves(both)
            factors[: 2 * rank, here] = high
            factors[2 * rank :, here] = low
            high_t, low_t = halves(both.T)
            factors_t[here, : 2 * rank] = high_t
            factors_t[here, 2 * rank :] = low_t
            total = None
        else:
            total = acc[here, :]
        highs, lows = [], []
        for k in range(blocks):
            if first:
                rating, seen = own_ratings[here, :], own_mask[here, :]
            else:
                columns = pl.ds(pl.multiple_of(where[k] * wide, wide), wide)
                rating, seen = ratings[here, columns], mask[here, columns]
            seen = seen.astype(F32)
            raw = dot(factors_t[here, :], forward[k]) + dot(factors_t[here, : 2 * rank], forward_low[k])
            seen = jnp.concatenate(
                [
                    seen[t * tile : (t + 1) * tile]
                    * (pattern[where[k], step // tile + t].astype(F32) * (1.0 / 64.0))
                    for t in range(rows // tile)
                ],
                axis=0,
            )
            res = seen * (raw[:, :wide] - rating)
            change = seen * raw[:, wide:]
            rc_high, rc_low = halves(jnp.concatenate([res, change], axis=1))
            out = dot(rc_high, back[k])
            out = out[:, : 2 * rank] + out[:, 2 * rank :] + dot(rc_low, back[k, :, : 2 * rank])
            total = out if total is None else total + out
            highs.append(rc_high)
            lows.append(rc_low)
        f = factors[:, here]
        got = dot(f, jnp.concatenate(highs, axis=1))
        got = got[: 2 * rank] + got[2 * rank :] + dot(f[: 2 * rank], jnp.concatenate(lows, axis=1))
        for k in range(blocks):
            items[k][:rank] += got[:rank, 2 * k * wide : (2 * k + 1) * wide]
            items[k][rank:] += got[:rank, (2 * k + 1) * wide : (2 * k + 2) * wide] + got[rank:, 2 * k * wide : (2 * k + 1) * wide]
        if last:
            user = total.T
            there = pl.ds(step - start, rows)
            keep[:, there] = user[:rank]
            send[:, there] = user[rank:]
            turned = own_first(left_dir[:, here])
            curve[...] += tile_sum(turned[:half] * user[half:rank] + turned[half:] * user[rank + half :])
        else:
            acc_out[here, :] = total

    for s in range(start, stop, rows):
        do(s)
    if first:
        for copy in late:
            copy.wait()
    for k in range(blocks):
        curve[...] += tile_sum(items[k][rank:] * panels[k][rank:])


def block_call(where, pattern, ratings, mask, given, panels, first=False, last=False, span=None, rows=512, name="block"):
    users, width = ratings.shape
    rank = panels[0].shape[0] // 2
    wide = panels[0].shape[1]
    blocks = len(panels)
    span = span or (0, users)
    count = span[1] - span[0]
    shape = jax.ShapeDtypeStruct
    outs = []
    scratch = [
        pltpu.VMEM((blocks, 4 * rank, 2 * wide), BF16),
        pltpu.VMEM((blocks, 2 * rank, 2 * wide), BF16),
        pltpu.VMEM((blocks, 2 * wide, 4 * rank), BF16),
    ]
    if first:
        outs += [shape((users, 4 * rank), BF16), shape((4 * rank, users), BF16)]
        outs += [shape(x.shape, x.dtype) for x in (ratings, mask, given[1])]
        steps = users // rows
        scratch += [
            pltpu.VMEM((rank, users), F32),
            pltpu.VMEM((users, wide), ratings.dtype),
            pltpu.VMEM((users, wide), mask.dtype),
            pltpu.SemaphoreType.DMA((2, steps)),
            pltpu.SemaphoreType.DMA((2, steps)),
            pltpu.SemaphoreType.DMA((2, width // wide - 1)),
        ]
    outs += [shape((rank, count), F32)] * 2 if last else [shape((users, 2 * rank), F32)]
    outs += [shape((1, 128), F32)] + [shape((2 * rank, wide), F32)] * blocks
    args = [ratings, mask, *given, *panels]
    far = 4 if first else 0
    args = [pltpu.with_memory_space_constraint(a, pltpu.HBM) for a in args[:far]] + [pltpu.with_memory_space_constraint(a, pltpu.VMEM) for a in args[far:]]
    return pl.pallas_call(
        functools.partial(block_kernel, blocks, first, last, span, rows, users // pattern.shape[1]),
        in_specs=[SMEM, SMEM] + [HBM] * far + [VMEM] * (len(args) - far),
        out_specs=[VMEM] * len(outs),
        out_shape=outs,
        scratch_shapes=scratch,
        compiler_params=pltpu.CompilerParams(vmem_limit_bytes=24 * 1024 * 1024),
        cost_estimate=pl.CostEstimate(flops=2 * count * wide * blocks * rank * 54, bytes_accessed=8 * count * wide * blocks, transcendentals=0),
        name=name,
    )(where, pltpu.with_memory_space_constraint(pattern, pltpu.HBM), *args)


def items_kernel(count, *refs):
    terms, curves, (total, sums) = refs[:count], refs[count:-2], refs[-2:]
    x = functools.reduce(jnp.add, [t[...] for t in terms])
    total[...] = x
    grad = x[: x.shape[0] // 2]
    squares = jnp.sum(grad * grad, axis=0, keepdims=True)
    wide = squares.shape[1]
    if wide < 128:
        squares = jnp.concatenate([squares, jnp.zeros((1, 128 - wide), F32)], axis=1)
    curve = functools.reduce(jnp.add, [c[...] for c in curves])
    sums[...] = jnp.concatenate([squares, curve, jnp.zeros((6, 128), F32)], axis=0)


def parts_kernel(total, after, grad, hess):
    rank = grad.shape[0]
    grad[...] = total[:rank]
    hess[...] = total[rank:]


def parts_call(total, after):
    shape = (total.shape[0] // 2, total.shape[1])
    return small_call(parts_kernel, [total, after], [shape, shape], "parts")


def small_call(kernel, args, outs, name, flops=0):
    args = [pltpu.with_memory_space_constraint(a, pltpu.VMEM) for a in args]
    return pl.pallas_call(
        kernel,
        in_specs=[VMEM] * len(args),
        out_specs=[VMEM] * len(outs),
        out_shape=[jax.ShapeDtypeStruct(o, F32) for o in outs],
        compiler_params=pltpu.CompilerParams(vmem_limit_bytes=4 * 1024 * 1024),
        cost_estimate=pl.CostEstimate(flops=flops, bytes_accessed=0, transcendentals=0),
        name=name,
    )(*args)


def items_call(terms, curves):
    return small_call(
        functools.partial(items_kernel, len(terms)),
        [*terms, *curves],
        [terms[0].shape, (8, 128)],
        "items_total",
        HEAVY,
    )


def squares_kernel(copies, a, b, sums, total, new):
    x = a[...] + b[...]
    total[...] = x
    new[...] = sums[...]
    new[0:1] += tile_sum(x * x) * (1.0 / copies)


def squares_call(a, b, sums, copies):
    return small_call(functools.partial(squares_kernel, copies), [a, b, sums], [a.shape, sums.shape], "squares")


def add_kernel(a, b, after, total):
    total[...] = a[...] + b[...]


def add_call(a, b, after):
    return small_call(add_kernel, [a, b, after], [a.shape], "add")[0]


def inner_kernel(a, b, g, h, inner):
    x = a[...] + b[...]
    inner[0] = jnp.sum(x[0:1])
    inner[1] = jnp.sum(x[1:2])


def inner_call(a, b, g, h):
    a, b = (pltpu.with_memory_space_constraint(x, pltpu.VMEM) for x in (a, b))
    return pl.pallas_call(
        inner_kernel,
        in_specs=[VMEM, VMEM, HBM, HBM],
        out_specs=SMEM,
        out_shape=jax.ShapeDtypeStruct((2,), F32),
        compiler_params=pltpu.CompilerParams(vmem_limit_bytes=4 * 1024 * 1024),
        name="inner",
    )(a, b, g, h)


def swap(x, axis, bit):
    return lax.ppermute(x, axis, [(i, i ^ bit) for i in range(lax.axis_size(axis))])


def swap_both(x, users_bit, items_bit):
    users, items = lax.axis_size("users"), lax.axis_size("items")
    pairs = [(u * items + i, (u ^ users_bit) * items + (i ^ items_bit)) for u in range(users) for i in range(items)]
    return lax.ppermute(x, ("users", "items"), pairs)


def bits(axis):
    return [1 << i for i in range(lax.axis_size(axis).bit_length() - 1)]


def per_device(ratings, entry_mask, pattern, left, left_dir, right, right_dir):
    rank = left.shape[1]
    wide = right.shape[0]
    n = lax.axis_size("users")
    me = lax.axis_index("users")
    core = lax.axis_index("items") % 2
    own = jnp.concatenate([right.T, right_dir.T], axis=0)
    direct = wide == 128
    if direct:
        panels = [own] + [swap(own, "users", k) for k in range(1, n)]
        index = [me ^ k for k in range(n)]
    else:
        panel = lax.all_gather(own, "users", axis=1, tiled=True)
        panels = [panel[:, i : i + 128] for i in range(0, panel.shape[1], 128)]
        index = list(range(len(panels)))

    def where(blocks):
        return jnp.stack([jnp.asarray(i, jnp.int32) for i in [index[k] for k in blocks] + [core]])

    table = pattern.T
    factors_t, factors, ratings, entry_mask, left_dir_t, acc, curve_a, item = block_call(
        where(range(len(panels))), table, ratings, entry_mask, [left.T, left_dir.T], panels[:1],
        first=True, rows=512, name="own_block",
    )
    others = list(range(1, len(panels)))
    keep, send, curve_b, *rest = block_call(
        where(others), table, ratings, entry_mask, [factors_t, factors, acc, left_dir_t], panels[1:],
        last=True, rows=2048, name="other_blocks",
    )
    items = [item, *rest]
    got = swap(send, "items", 1)
    half = rank // 2
    g = keep[:half] + got[:half]
    h = keep[half:] + got[half:]
    across = bits("items")[1:]
    for bit in across[:-1]:
        g = g + swap(g, "items", bit)
        h = h + swap(h, "items", bit)
    other_g = swap(g, "items", across[-1])
    other_h = swap(h, "items", across[-1])
    if direct:
        terms = [items[0]] + [swap(items[k], "users", k) for k in [2,3,1]]
    else:
        terms = [
            lax.psum_scatter(jnp.concatenate(items, axis=1), "users", scatter_dimension=1, tiled=True)
        ]
    total, sums = items_call(terms, [curve_a, curve_b])
    for bit in across:
        sums = sums + swap(sums, "items", bit)
    g, sums = squares_call(g, other_g, sums, 1)
    h = add_call(h, other_h, sums)
    grad_right, hess_right = parts_call(total, sums)
    for bit in bits("users"):
        sums = sums + swap(sums, "users", bit)
    far = swap(sums, "items", 1)

    def joined(mine):
        other = swap(mine, "items", 1)
        return jnp.concatenate([jnp.where(core == 0, mine, other), jnp.where(core == 0, other, mine)], axis=0)

    g, h = joined(g), joined(h)
    inner = inner_call(sums, far, g, h)
    return g.T, h.T, grad_right.T, hess_right.T, inner


def solution(mesh):
    placed = (
        P(("copies", "users"), "items"),
        P(("copies", "users"), "items"),
        P(("copies", "users"), "items"),
        P(("copies", "users"), None),
        P(("copies", "users"), None),
        P(("copies", "items", "users"), None),
        P(("copies", "items", "users"), None),
    )
    return jax.shard_map(
        per_device,
        mesh=mesh,
        in_specs=placed,
        out_specs=(
            P(("copies", "users"), None),
            P(("copies", "users"), None),
            P(("copies", "items", "users"), None),
            P(("copies", "items", "users"), None),
            P("copies"),
        ),
        check_vma=False,
    )
```

```python
import functools
import itertools
import jax
import jax.numpy as jnp
from jax import lax
from jax.experimental import pallas as pl
from jax.experimental.pallas import tpu as pltpu
from jax.sharding import PartitionSpec as P

F32 = jnp.float32
BF16 = jnp.bfloat16
HEAVY = 20_000_000_000
SMEM = pl.BlockSpec(memory_space=pltpu.SMEM)
VMEM = pl.BlockSpec(memory_space=pltpu.VMEM)
HBM = pl.BlockSpec(memory_space=pltpu.HBM)


def dot(a, b):
    return jnp.dot(a, b, preferred_element_type=F32)


def halves(x):
    high = x.astype(BF16)
    return high, (x - high.astype(F32)).astype(BF16)


def tile_sum(x):
    total = jnp.sum(x, axis=0, keepdims=True)
    return functools.reduce(jnp.add, [total[:, i : i + 128] for i in range(0, total.shape[1], 128)])


def first_loads(where, rows, factors, factors_to, factor_sems, grids, grids_to, own_sems):
    users, width = grids[0].shape
    wide = 128
    block = lambda k: pl.ds(pl.multiple_of(where[k] * wide, wide), wide)
    steps = []
    for step in range(users // rows):
        here = pl.ds(step * rows, rows)
        steps.append(
            [
                pltpu.make_async_copy(a.at[:, here], b.at[:, here], factor_sems.at[i, step])
                for i, (a, b) in enumerate(zip(factors, factors_to))
            ]
            + [
                pltpu.make_async_copy(a.at[here, block(0)], b.at[here], own_sems.at[i, step])
                for i, (a, b) in enumerate(zip(grids, grids_to))
            ]
        )
    return steps


def other_loads(where, blocks, here, grids, grids_to, sems):
    wide = 128
    block = lambda k: pl.ds(pl.multiple_of(where[k] * wide, wide), wide)
    return [
        pltpu.make_async_copy(a.at[here, block(k)], b.at[:, block(k)], sems.at[i, j])
        for j, k in enumerate(blocks)
        for i, (a, b) in enumerate(zip(grids, grids_to))
    ]


def block_kernel(blocks, first, last, span, rows, tile, where, pattern, ratings, mask, *refs):
    refs = list(refs)
    take = lambda n: [refs.pop(0) for _ in range(n)]
    if first:
        left_hbm, left_dir_hbm = take(2)
    else:
        factors_t, factors, acc = take(3)
        left_dir = take(1)[0] if last else None
    panels = take(blocks)
    start, stop = span
    if first:
        factors_t, factors, all_ratings, all_mask, left_dir = take(5)
    if last:
        keep, send = take(2)
    else:
        acc_out = take(1)[0]
    curve = take(1)[0]
    items = take(blocks)
    forward, forward_low, back = take(3)
    if first:
        left, own_ratings, own_mask, factor_sems, own_sems, other_sems = refs
        loads = first_loads(
            where, rows, (left_hbm, left_dir_hbm), (left, left_dir), factor_sems,
            (ratings, mask), (own_ratings, own_mask), own_sems,
        )
        late = other_loads(
            where, range(1, ratings.shape[1] // 128), pl.ds(0, mask.shape[0]),
            (ratings, mask), (all_ratings, all_mask), other_sems,
        )
        for copy in itertools.chain(*loads, late):
            copy.start()
    rank2, wide = panels[0].shape
    rank = rank2 // 2
    half = rank // 2
    flip = where[ratings.shape[1] // wide] == 1
    base = 0 if first else 1

    def own_first(x):
        return jnp.where(flip, jnp.concatenate([x[half:], x[:half]], axis=0), x)

    for k in range(blocks):
        p, d = panels[k][:rank], panels[k][rank:]
        zero = jnp.zeros_like(p)
        q = jnp.concatenate([jnp.concatenate([p, d], axis=1), jnp.concatenate([zero, p], axis=1)], axis=0)
        high, low = halves(q)
        forward[k, : 2 * rank] = high
        forward[k, 2 * rank :] = high
        forward_low[k] = low
        p, d, zero = own_first(p), own_first(d), zero[:half]
        s = jnp.concatenate(
            [
                jnp.concatenate([p[:half], zero], axis=1),
                jnp.concatenate([d[:half], p[:half]], axis=1),
                jnp.concatenate([p[half:], zero], axis=1),
                jnp.concatenate([d[half:], p[half:]], axis=1),
            ],
            axis=0,
        ).T
        high, low = halves(s)
        back[k, :, : 2 * rank] = high
        back[k, :, 2 * rank :] = low
        items[k][...] = jnp.zeros_like(items[k])
    curve[...] = jnp.zeros_like(curve)

    def do(step):
        here = pl.ds(step, rows)
        if first:
            for copy in loads[step // rows]:
                copy.wait()
            both = jnp.concatenate([left[:, here], left_dir[:, here]], axis=0)
            high, low = halves(both)
            factors[: 2 * rank, here] = high
            factors[2 * rank :, here] = low
            high_t, low_t = halves(both.T)
            factors_t[here, : 2 * rank] = high_t
            factors_t[here, 2 * rank :] = low_t
            total = None
        else:
            total = acc[here, :]
        highs, lows = [], []
        for k in range(blocks):
            if first:
                rating, seen = own_ratings[here, :], own_mask[here, :]
            else:
                columns = pl.ds(pl.multiple_of(where[base + k] * wide, wide), wide)
                rating, seen = ratings[here, columns], mask[here, columns]
            seen = seen.astype(F32)
            raw = dot(factors_t[here, :], forward[k]) + dot(factors_t[here, : 2 * rank], forward_low[k])
            seen = jnp.concatenate(
                [
                    seen[t * tile : (t + 1) * tile]
                    * (pattern[where[base + k], step // tile + t].astype(F32) * (1.0 / 64.0))
                    for t in range(rows // tile)
                ],
                axis=0,
            )
            res = seen * (raw[:, :wide] - rating)
            change = seen * raw[:, wide:]
            rc_high, rc_low = halves(jnp.concatenate([res, change], axis=1))
            out = dot(rc_high, back[k])
            out = out[:, : 2 * rank] + out[:, 2 * rank :] + dot(rc_low, back[k, :, : 2 * rank])
            total = out if total is None else total + out
            highs.append(rc_high)
            lows.append(rc_low)
        f = factors[:, here]
        got = dot(f, jnp.concatenate(highs, axis=1))
        got = got[: 2 * rank] + got[2 * rank :] + dot(f[: 2 * rank], jnp.concatenate(lows, axis=1))
        for k in range(blocks):
            items[k][:rank] += got[:rank, 2 * k * wide : (2 * k + 1) * wide]
            items[k][rank:] += got[:rank, (2 * k + 1) * wide : (2 * k + 2) * wide] + got[rank:, 2 * k * wide : (2 * k + 1) * wide]
        if last:
            user = total.T
            there = pl.ds(step - start, rows)
            keep[:, there] = user[:rank]
            send[:, there] = user[rank:]
            turned = own_first(left_dir[:, here])
            curve[...] += tile_sum(turned[:half] * user[half:rank] + turned[half:] * user[rank + half :])
        else:
            acc_out[here, :] = total

    for s in range(start, stop, rows):
        do(s)
    if first:
        for copy in late:
            copy.wait()
    for k in range(blocks):
        curve[...] += tile_sum(items[k][rank:] * panels[k][rank:])


def block_call(where, pattern, ratings, mask, given, panels, first=False, last=False, span=None, rows=512, name="block"):
    users, width = ratings.shape
    rank = panels[0].shape[0] // 2
    wide = panels[0].shape[1]
    blocks = len(panels)
    span = span or (0, users)
    count = span[1] - span[0]
    shape = jax.ShapeDtypeStruct
    outs = []
    scratch = [
        pltpu.VMEM((blocks, 4 * rank, 2 * wide), BF16),
        pltpu.VMEM((blocks, 2 * rank, 2 * wide), BF16),
        pltpu.VMEM((blocks, 2 * wide, 4 * rank), BF16),
    ]
    if first:
        outs += [shape((users, 4 * rank), BF16), shape((4 * rank, users), BF16)]
        outs += [shape(x.shape, x.dtype) for x in (ratings, mask, given[1])]
        steps = users // rows
        scratch += [
            pltpu.VMEM((rank, users), F32),
            pltpu.VMEM((users, wide), ratings.dtype),
            pltpu.VMEM((users, wide), mask.dtype),
            pltpu.SemaphoreType.DMA((2, steps)),
            pltpu.SemaphoreType.DMA((2, steps)),
            pltpu.SemaphoreType.DMA((2, width // wide - 1)),
        ]
    outs += [shape((rank, count), F32)] * 2 if last else [shape((users, 2 * rank), F32)]
    outs += [shape((1, 128), F32)] + [shape((2 * rank, wide), F32)] * blocks
    args = [ratings, mask, *given, *panels]
    far = 4 if first else 0
    args = [pltpu.with_memory_space_constraint(a, pltpu.HBM) for a in args[:far]] + [pltpu.with_memory_space_constraint(a, pltpu.VMEM) for a in args[far:]]
    return pl.pallas_call(
        functools.partial(block_kernel, blocks, first, last, span, rows, users // pattern.shape[1]),
        in_specs=[SMEM, SMEM] + [HBM] * far + [VMEM] * (len(args) - far),
        out_specs=[VMEM] * len(outs),
        out_shape=outs,
        scratch_shapes=scratch,
        compiler_params=pltpu.CompilerParams(vmem_limit_bytes=24 * 1024 * 1024),
        cost_estimate=pl.CostEstimate(flops=2 * count * wide * blocks * rank * 54, bytes_accessed=8 * count * wide * blocks, transcendentals=0),
        name=name,
    )(where, pltpu.with_memory_space_constraint(pattern, pltpu.HBM), *args)


def items_kernel(count, *refs):
    terms, curves, (total, sums) = refs[:count], refs[count:-2], refs[-2:]
    x = functools.reduce(jnp.add, [t[...] for t in terms])
    total[...] = x
    grad = x[: x.shape[0] // 2]
    squares = jnp.sum(grad * grad, axis=0, keepdims=True)
    wide = squares.shape[1]
    if wide < 128:
        squares = jnp.concatenate([squares, jnp.zeros((1, 128 - wide), F32)], axis=1)
    curve = functools.reduce(jnp.add, [c[...] for c in curves])
    sums[...] = jnp.concatenate([squares, curve, jnp.zeros((6, 128), F32)], axis=0)


def parts_kernel(total, after, grad, hess):
    rank = grad.shape[0]
    grad[...] = total[:rank]
    hess[...] = total[rank:]


def parts_call(total, after):
    shape = (total.shape[0] // 2, total.shape[1])
    return small_call(parts_kernel, [total, after], [shape, shape], "parts")


def small_call(kernel, args, outs, name, flops=0):
    args = [pltpu.with_memory_space_constraint(a, pltpu.VMEM) for a in args]
    return pl.pallas_call(
        kernel,
        in_specs=[VMEM] * len(args),
        out_specs=[VMEM] * len(outs),
        out_shape=[jax.ShapeDtypeStruct(o, F32) for o in outs],
        compiler_params=pltpu.CompilerParams(vmem_limit_bytes=4 * 1024 * 1024),
        cost_estimate=pl.CostEstimate(flops=flops, bytes_accessed=0, transcendentals=0),
        name=name,
    )(*args)


def items_call(terms, curves):
    return small_call(
        functools.partial(items_kernel, len(terms)),
        [*terms, *curves],
        [terms[0].shape, (8, 128)],
        "items_total",
        HEAVY,
    )


def squares_kernel(copies, a, b, sums, total, new):
    x = a[...] + b[...]
    total[...] = x
    new[...] = sums[...]
    new[0:1] += tile_sum(x * x) * (1.0 / copies)


def squares_call(a, b, sums, copies):
    return small_call(functools.partial(squares_kernel, copies), [a, b, sums], [a.shape, sums.shape], "squares")


def add_kernel(a, b, after, total):
    total[...] = a[...] + b[...]


def add_call(a, b, after):
    return small_call(add_kernel, [a, b, after], [a.shape], "add")[0]


def inner_kernel(a, b, g, h, inner):
    x = a[...] + b[...]
    inner[0] = jnp.sum(x[0:1])
    inner[1] = jnp.sum(x[1:2])


def inner_call(a, b, g, h):
    a, b = (pltpu.with_memory_space_constraint(x, pltpu.VMEM) for x in (a, b))
    return pl.pallas_call(
        inner_kernel,
        in_specs=[VMEM, VMEM, HBM, HBM],
        out_specs=SMEM,
        out_shape=jax.ShapeDtypeStruct((2,), F32),
        compiler_params=pltpu.CompilerParams(vmem_limit_bytes=4 * 1024 * 1024),
        name="inner",
    )(a, b, g, h)


def swap(x, axis, bit):
    return lax.ppermute(x, axis, [(i, i ^ bit) for i in range(lax.axis_size(axis))])


def swap_both(x, users_bit, items_bit):
    users, items = lax.axis_size("users"), lax.axis_size("items")
    pairs = [(u * items + i, (u ^ users_bit) * items + (i ^ items_bit)) for u in range(users) for i in range(items)]
    return lax.ppermute(x, ("users", "items"), pairs)


def bits(axis):
    return [1 << i for i in range(lax.axis_size(axis).bit_length() - 1)]


def per_device(ratings, entry_mask, pattern, left, left_dir, right, right_dir):
    rank = left.shape[1]
    wide = right.shape[0]
    n = lax.axis_size("users")
    me = lax.axis_index("users")
    core = lax.axis_index("items") % 2
    own = jnp.concatenate([right.T, right_dir.T], axis=0)
    direct = wide == 128
    if direct:
        panels = [own] + [swap(own, "users", k) for k in range(1, n)]
        index = [me ^ k for k in range(n)]
    else:
        panel = lax.all_gather(own, "users", axis=1, tiled=True)
        panels = [panel[:, i : i + 128] for i in range(0, panel.shape[1], 128)]
        index = list(range(len(panels)))

    where = jnp.stack([jnp.asarray(i, jnp.int32) for i in [*index, core]])
    table = pattern.T
    factors_t, factors, ratings, entry_mask, left_dir_t, acc, curve_a, item = block_call(
        where, table, ratings, entry_mask, [left.T, left_dir.T], panels[:1],
        first=True, rows=512, name="own_block",
    )
    keep, send, curve_b, *rest = block_call(
        where, table, ratings, entry_mask, [factors_t, factors, acc, left_dir_t], panels[1:],
        last=True, rows=2048, name="other_blocks",
    )
    items = [item, *rest]
    got = swap(send, "items", 1)
    half = rank // 2
    g = keep[:half] + got[:half]
    h = keep[half:] + got[half:]
    across = bits("items")[1:]
    for bit in across[:-1]:
        g = g + swap(g, "items", bit)
        h = h + swap(h, "items", bit)
    other_g = swap(g, "items", across[-1])
    other_h = swap(h, "items", across[-1])
    if direct:
        terms = [items[0]] + [swap(items[k], "users", k) for k in [2,3,1]]
    else:
        terms = [
            lax.psum_scatter(jnp.concatenate(items, axis=1), "users", scatter_dimension=1, tiled=True)
        ]
    total, sums = items_call(terms, [curve_a, curve_b])
    for bit in across:
        sums = sums + swap(sums, "items", bit)
    g, sums = squares_call(g, other_g, sums, 1)
    h = add_call(h, other_h, sums)
    grad_right, hess_right = parts_call(total, sums)
    for bit in bits("users"):
        sums = sums + swap(sums, "users", bit)
    far = swap(sums, "items", 1)

    def joined(mine):
        other = swap(mine, "items", 1)
        return jnp.concatenate([jnp.where(core == 0, mine, other), jnp.where(core == 0, other, mine)], axis=0)

    g, h = joined(g), joined(h)
    inner = inner_call(sums, far, g, h)
    return g.T, h.T, grad_right.T, hess_right.T, inner


def solution(mesh):
    placed = (
        P(("copies", "users"), "items"),
        P(("copies", "users"), "items"),
        P(("copies", "users"), "items"),
        P(("copies", "users"), None),
        P(("copies", "users"), None),
        P(("copies", "items", "users"), None),
        P(("copies", "items", "users"), None),
    )
    return jax.shard_map(
        per_device,
        mesh=mesh,
        in_specs=placed,
        out_specs=(
            P(("copies", "users"), None),
            P(("copies", "users"), None),
            P(("copies", "items", "users"), None),
            P(("copies", "items", "users"), None),
            P("copies"),
        ),
        check_vma=False,
    )
```
